256 devices in a mesh: row: 16 (over z, x_hi), col: 16 (over x_lo, y, core).
Axes of the slice: x: 4 (x_hi: 2, x_lo: 2; x = x_hi * 2 + x_lo), y: 4, z: 8, core: 2. Of those that a mesh axis runs over, the one named last changes fastest.
Arguments:
- pair: bfloat16 [512, 512, 128], P('row', 'col'), may hold values from -6 to 6
- cotangent: bfloat16 [512, 512, 128], P('row', 'col'), may hold values from -6 to 6
- chain_counts: int32 [4], replicated, may hold values from 1 to 256, 512 in all
- crop_skip: int32 [4], replicated, may hold values from 0 to 31
- w_proj: bfloat16 [128, 256], replicated, may hold values from -0.5 to 0.5
- w_gate_in: bfloat16 [128, 256], replicated, may hold values from -0.5 to 0.5
- w_gate_out: bfloat16 [128, 128], replicated, may hold values from -0.5 to 0.5
- w_out: bfloat16 [128, 128], replicated, may hold values from -0.5 to 0.5
Outputs:
- updated: bfloat16 [512, 512, 128], P('row', 'col')
- grad_pair: bfloat16 [512, 512, 128], P('row', 'col')
- grad_proj: float32 [128, 256], replicated
- grad_gate_in: float32 [128, 256], replicated
- grad_gate_out: float32 [128, 128], replicated
- grad_out: float32 [128, 128], replicated
The draws below stay inside these ranges and needn't reach their ends.
Inputs may be any that keep to these rules, and one draw needn't show every extreme that they name: `chain_counts`: the counts sum to 512.
All inputs are finite; a program needn't handle non-finite values.
Results may differ from the reference program's by a relative error of at most 0.0093.
Values may be sent and summed in bfloat16 or wider, within the bound.
A program may use at most 128 MiB of HBM per device.

```python
import math
import jax
import jax.numpy as jnp
import numpy as np
from jax import lax

C = 128
H = 128
R_DEV = 32
CHAINS = 4
N = 512


def touch_ends(entries, stream_key, smallest, high):
    spot = [jax.random.randint(jax.random.fold_in(stream_key, axis), (), 0, length) for axis, length in enumerate(entries.shape)]
    longest = entries.shape.index(max(entries.shape))
    next_to = spot[:longest] + [(spot[longest] + 1) % entries.shape[longest]] + spot[longest + 1:]
    return entries.at[tuple(spot)].set(smallest).at[tuple(next_to)].set(high)


def levels(key, shape, split, least, largest):
    level = 1.0
    for dim, shards_of in split:
        draws = jax.random.uniform(jax.random.fold_in(jax.random.fold_in(key, 6), dim), (shards_of,), jnp.float32, least / len(split), largest / len(split))
        level = level * jnp.repeat(jnp.exp(draws), shape[dim] // shards_of).reshape((-1,) + (1,) * (len(shape) - 1 - dim))
    return level


def length_profile(amount, total, bound, slope):
    portions = [(1 << 20) // math.isqrt(grade ** slope) + 1 for grade in range(2, amount + 1)]
    rest, given = total - bound - (amount - 1), [1] * (amount - 1)
    while rest > 0:
        candidates = [i for i in range(amount - 1) if given[i] < bound]
        mass, budget = sum([portions[i] for i in candidates]), rest
        for i in candidates:
            addition = min(bound - given[i], max(1, budget * portions[i] // mass), rest)
            given[i] = given[i] + addition
            rest = rest - addition
    return np.array([bound] + given)


def ragged(key, amount, total, most, slope):
    if amount == 2:
        one = jax.random.randint(key, (), max(1, total - most), min(most, total - 1) + 1)
        return jnp.stack([one, total - one])
    tallies = jnp.asarray(length_profile(amount, total, most, slope), jnp.int32)
    twos = (amount - 1) // 2
    source_of, receiver = tallies[1:1 + 2 * twos:2], tallies[2:2 + 2 * twos:2]
    slack = jnp.minimum(source_of - 1, most - receiver)
    moved = jax.random.randint(jax.random.fold_in(key, 1), (twos,), 0, 1 << 20) % (slack + 1)
    tallies = tallies.at[1:1 + 2 * twos:2].set(source_of - moved).at[2:2 + 2 * twos:2].set(receiver + moved)
    return tallies[jax.random.permutation(jax.random.fold_in(key, 2), amount)]


def gaussian(rng, extent, deviation, most, shards=(), kind=jnp.bfloat16):
    entries = deviation * jax.random.normal(rng, extent, jnp.float32)
    if shards:
        entries = entries * levels(rng, extent, shards, -0.22, 0.18)
    return jnp.clip(entries, -most, most).astype(kind)


def setup_inputs(seed: int = 0) -> dict:
    arg_keys = jax.random.split(jax.random.key(seed), 9)
    pair = gaussian(arg_keys[0], (N, N, C), 1.0, 6.0, ((0, 16), (1, 16)))
    cotangent = gaussian(arg_keys[1], (N, N, C), 1.0, 6.0, ((0, 16), (1, 16)))
    chain_counts = ragged(arg_keys[2], CHAINS, N, N // 2, 1).astype(jnp.int32)
    crop_skip = touch_ends(jax.random.randint(arg_keys[3], (CHAINS,), 0, R_DEV), jax.random.fold_in(arg_keys[3], 1), 0, R_DEV - 1).astype(jnp.int32)
    w_proj = gaussian(arg_keys[4], (C, 2 * H), C ** -0.5, 0.5)
    w_gate_in = gaussian(arg_keys[5], (C, 2 * H), C ** -0.5, 0.5)
    w_gate_out = gaussian(arg_keys[6], (C, C), C ** -0.5, 0.5)
    w_out = gaussian(arg_keys[7], (H, C), H ** -0.5, 0.5)
    return {"pair": pair, "cotangent": cotangent, "chain_counts": chain_counts, "crop_skip": crop_skip, "w_proj": w_proj, "w_gate_in": w_gate_in, "w_gate_out": w_gate_out, "w_out": w_out}


def residue_valid(index, chain_counts, crop_skip):
    ends = jnp.cumsum(chain_counts)
    starts = ends - chain_counts
    place = index[:, None]
    inside = (place >= starts[None, :]) & (place < ends[None, :]) & (place - starts[None, :] >= crop_skip[None, :])
    return jnp.any(inside, axis=1).astype(jnp.float32)

def reference(pair, cotangent, chain_counts, crop_skip, w_proj, w_gate_in, w_gate_out, w_out):
    hidden = w_out.shape[0]
    index = jnp.arange(N, dtype=jnp.int32)
    valid = residue_valid(index, chain_counts, crop_skip)
    cell_mask = (valid[:, None] * valid[None, :])[..., None]
    pair_float_input = pair.astype(jnp.float32)
    channel_mean = lax.optimization_barrier(jnp.mean(pair_float_input, axis=-1, keepdims=True))
    var = lax.optimization_barrier(jnp.mean((pair_float_input - channel_mean) ** 2, axis=-1, keepdims=True))
    inverse_deviation = 1.0 / jnp.sqrt(var + 1e-05)
    normalized_input = (pair_float_input - channel_mean) * inverse_deviation
    pair_input = normalized_input.astype(jnp.bfloat16)
    s_proj = jnp.dot(pair_input, w_proj, preferred_element_type=jnp.float32)
    s_gate = jnp.dot(pair_input, w_gate_in, preferred_element_type=jnp.float32)
    sig = jax.nn.sigmoid(s_gate)
    both = cell_mask * sig * s_proj
    left = both[..., :hidden].astype(jnp.bfloat16)
    right = both[..., hidden:].astype(jnp.bfloat16)
    tri = jnp.einsum('ikh,jkh->ijh', left.astype(jnp.float32), right.astype(jnp.float32))
    tmean = lax.optimization_barrier(jnp.mean(tri, axis=-1, keepdims=True))
    tvar = lax.optimization_barrier(jnp.mean((tri - tmean) ** 2, axis=-1, keepdims=True))
    trstd = 1.0 / jnp.sqrt(tvar + 1e-05)
    that = (tri - tmean) * trstd
    tnorm = that.astype(jnp.bfloat16)
    gout = jax.nn.sigmoid(jnp.dot(pair_input, w_gate_out, preferred_element_type=jnp.float32))
    y_proj = jnp.dot(tnorm, w_out, preferred_element_type=jnp.float32)
    updated = (pair_float_input + gout * y_proj).astype(jnp.bfloat16)
    ct_f = cotangent.astype(jnp.float32)
    d_y = (ct_f * gout).astype(jnp.bfloat16)
    d_sgout = (ct_f * y_proj * gout * (1.0 - gout)).astype(jnp.bfloat16)
    d_tnorm = jnp.einsum('ijc,hc->ijh', d_y.astype(jnp.float32), w_out.astype(jnp.float32))
    d_tri = (trstd * (d_tnorm - lax.optimization_barrier(jnp.mean(d_tnorm, axis=-1, keepdims=True)) - that * lax.optimization_barrier(jnp.mean(d_tnorm * that, axis=-1, keepdims=True)))).astype(jnp.bfloat16)
    d_tri_f = d_tri.astype(jnp.float32)
    d_left = jnp.einsum('ijh,jkh->ikh', d_tri_f, right.astype(jnp.float32))
    d_right = jnp.einsum('ijh,ikh->jkh', d_tri_f, left.astype(jnp.float32))
    d_both = jnp.concatenate([d_left, d_right], axis=-1)
    d_proj = (d_both * cell_mask * sig).astype(jnp.bfloat16)
    d_gate = (d_both * cell_mask * s_proj * sig * (1.0 - sig)).astype(jnp.bfloat16)
    input_gradient = jnp.einsum('ijh,ch->ijc', d_proj.astype(jnp.float32), w_proj.astype(jnp.float32))
    input_gradient = input_gradient + jnp.einsum('ijh,ch->ijc', d_gate.astype(jnp.float32), w_gate_in.astype(jnp.float32))
    input_gradient = input_gradient + jnp.einsum('ijd,cd->ijc', d_sgout.astype(jnp.float32), w_gate_out.astype(jnp.float32))
    gradient_before_norm = inverse_deviation * (input_gradient - lax.optimization_barrier(jnp.mean(input_gradient, axis=-1, keepdims=True)) - normalized_input * lax.optimization_barrier(jnp.mean(input_gradient * normalized_input, axis=-1, keepdims=True)))
    grad_pair = (ct_f + gradient_before_norm).astype(jnp.bfloat16)
    x_f = pair_input.astype(jnp.float32)
    grad_proj = jnp.einsum('ijc,ijh->ch', x_f, d_proj.astype(jnp.float32)) / N
    grad_gate_in = jnp.einsum('ijc,ijh->ch', x_f, d_gate.astype(jnp.float32)) / N
    grad_gate_out = jnp.einsum('ijc,ijd->cd', x_f, d_sgout.astype(jnp.float32)) / N
    grad_out = jnp.einsum('ijh,ijc->hc', tnorm.astype(jnp.float32), d_y.astype(jnp.float32)) / N
    return (updated, grad_pair, grad_proj, grad_gate_in, grad_gate_out, grad_out)
```

```python
import functools

import jax
import jax.numpy as jnp
from jax import lax
from jax.experimental import pallas as pl
from jax.experimental.pallas import tpu as pltpu
from jax.sharding import PartitionSpec as P

MESH = pl.DeviceIdType.MESH
BF = jnp.bfloat16
F32 = jnp.float32


def enter(r, c, sem):
    barrier = pltpu.get_barrier_semaphore()

    def greet(s, _):
        pl.semaphore_signal(barrier, inc=1, device_id=(lax.rem(r + s, 16), c), device_id_type=MESH)
        pl.semaphore_signal(barrier, inc=1, device_id=(r, lax.rem(c + s, 16)), device_id_type=MESH)
        return 0

    lax.fori_loop(1, 16, greet, 0)
    pl.semaphore_wait(barrier, 30)

    def tell(s, _):
        pl.semaphore_signal(sem, inc=1, device_id=(r, lax.rem(c + s, 16)), device_id_type=MESH)
        return 0

    lax.fori_loop(1, 16, tell, 0)
    pl.semaphore_wait(sem, 15)


def to_channels(src, full, send_sem, recv_sem, swap_send, swap_recv, r, c):
    half = r // 8
    m = c // 2
    core = lax.rem(c, 2)
    slot = r * 16 + c
    own = r * 8 + m
    same = core == half

    @pl.when(same)
    def _():
        pltpu.make_async_copy(src.at[own], full.at[slot], recv_sem).start()

    @pl.when(jnp.logical_not(same))
    def _():
        pltpu.make_async_remote_copy(
            src_ref=src.at[own], dst_ref=full.at[slot], send_sem=send_sem, recv_sem=recv_sem,
            device_id=(r, m * 2 + half), device_id_type=MESH,
        ).start()

    def body(s, _):
        r2 = lax.rem(r + lax.rem(s, 16), 16)
        m2 = lax.rem(m + s // 16, 8)
        pltpu.make_async_remote_copy(
            src_ref=src.at[r2 * 8 + m2], dst_ref=full.at[slot], send_sem=send_sem, recv_sem=recv_sem,
            device_id=(r2, m2 * 2 + half), device_id_type=MESH,
        ).start()
        return 0

    lax.fori_loop(1, 128, body, 0)
    mine = full.at[pl.ds(core * 128, 128)]
    pltpu.make_async_copy(mine, mine, recv_sem).wait()
    swap = pltpu.make_async_remote_copy(
        src_ref=mine, dst_ref=mine, send_sem=swap_send, recv_sem=swap_recv,
        device_id=(r, m * 2 + 1 - core), device_id_type=MESH,
    )
    swap.start()

    @pl.when(same)
    def _():
        pltpu.make_async_copy(src.at[pl.ds(0, 127)], src.at[pl.ds(0, 127)], send_sem).wait()

    @pl.when(jnp.logical_not(same))
    def _():
        pltpu.make_async_copy(src, src, send_sem).wait()

    swap.wait()


def to_cells(src, dst, send_sem, recv_sem, r, c):
    m = c // 2
    core = lax.rem(c, 2)
    channel = r * 8 + m
    home = core == r // 8

    @pl.when(home)
    def _():
        pltpu.make_async_copy(src.at[lax.rem(r, 8) * 16 + c], dst.at[channel], recv_sem).start()

    @pl.when(jnp.logical_not(home))
    def _():
        r2 = core * 8 + lax.rem(r, 8)
        pltpu.make_async_remote_copy(
            src_ref=src.at[lax.rem(r, 8) * 16 + c], dst_ref=dst.at[channel], send_sem=send_sem, recv_sem=recv_sem,
            device_id=(r2, c), device_id_type=MESH,
        ).start()

    def body(s, _):
        q = lax.rem(r + lax.rem(s, 8), 8)
        c2 = lax.rem(c + s // 8, 16)
        pltpu.make_async_remote_copy(
            src_ref=src.at[q * 16 + c2], dst_ref=dst.at[channel], send_sem=send_sem, recv_sem=recv_sem,
            device_id=(core * 8 + q, c2), device_id_type=MESH,
        ).start()
        return 0

    lax.fori_loop(1, 128, body, 0)
    pltpu.make_async_copy(dst, dst, recv_sem).wait()

    @pl.when(home)
    def _():
        pltpu.make_async_copy(src.at[pl.ds(0, 127)], src.at[pl.ds(0, 127)], send_sem).wait()

    @pl.when(jnp.logical_not(home))
    def _():
        pltpu.make_async_copy(src, src, send_sem).wait()


def channels_kernel(src, full, dma, reg):
    r, c = lax.axis_index("row"), lax.axis_index("col")
    enter(r, c, reg.at[0])
    to_channels(src, full, dma.at[0], dma.at[1], dma.at[2], dma.at[3], r, c)


def cells_kernel(src, dst, dma, reg):
    r, c = lax.axis_index("row"), lax.axis_index("col")
    enter(r, c, reg.at[0])
    to_cells(src, dst, dma.at[0], dma.at[1], r, c)


def sum_kernel(src, out, got, part, tot, parts, dma, reg):
    r, c = lax.axis_index("row"), lax.axis_index("col")
    enter(r, c, reg.at[0])

    def scatter(s, _):
        c2 = lax.rem(c + s, 16)
        pltpu.make_async_remote_copy(
            src_ref=src.at[c2], dst_ref=got.at[c], send_sem=dma.at[0], recv_sem=dma.at[1],
            device_id=(r, c2), device_id_type=MESH,
        ).start()
        return 0

    pltpu.make_async_copy(src.at[c], got.at[c], dma.at[1]).start()
    lax.fori_loop(1, 16, scatter, 0)
    pltpu.make_async_copy(got, got, dma.at[1]).wait()
    part[...] = jnp.sum(got[...], axis=0)

    def share(s, _):
        r2 = lax.rem(r + s, 16)
        pltpu.make_async_remote_copy(
            src_ref=part, dst_ref=parts.at[r], send_sem=dma.at[2], recv_sem=dma.at[3],
            device_id=(r2, c), device_id_type=MESH,
        ).start()
        return 0

    pltpu.make_async_copy(part, parts.at[r], dma.at[3]).start()
    lax.fori_loop(1, 16, share, 0)
    pltpu.make_async_copy(parts, parts, dma.at[3]).wait()
    tot[...] = jnp.sum(parts[...], axis=0)

    def gather(s, _):
        c2 = lax.rem(c + s, 16)
        pltpu.make_async_remote_copy(
            src_ref=tot, dst_ref=out.at[c], send_sem=dma.at[4], recv_sem=dma.at[5],
            device_id=(r, c2), device_id_type=MESH,
        ).start()
        return 0

    pltpu.make_async_copy(tot, out.at[c], dma.at[5]).start()
    lax.fori_loop(1, 16, gather, 0)
    pltpu.make_async_copy(out, out, dma.at[5]).wait()
    most = got.at[pl.ds(0, 15)]
    for k in (0, 2, 4):
        pltpu.make_async_copy(most, most, dma.at[k]).wait()


def run(kernel, x, out_shape, cid, scratch=()):
    vmem = pl.BlockSpec(memory_space=pltpu.VMEM)
    return pl.pallas_call(
        kernel,
        out_shape=out_shape,
        in_specs=[vmem],
        out_specs=vmem,
        scratch_shapes=list(scratch) + [pltpu.SemaphoreType.DMA((6,)), pltpu.SemaphoreType.REGULAR((1,))],
        compiler_params=pltpu.CompilerParams(collective_id=cid, has_side_effects=True, vmem_limit_bytes=40 << 20),
    )(x)


def residue_valid(index, chain_counts, crop_skip):
    ends = jnp.cumsum(chain_counts)
    starts = ends - chain_counts
    place = index[:, None]
    inside = (
        (place >= starts[None, :])
        & (place < ends[None, :])
        & (place - starts[None, :] >= crop_skip[None, :])
    )
    return jnp.any(inside, axis=1).astype(F32)


def shards(pair, cotangent, chain_counts, crop_skip, w_proj, w_gate_in, w_gate_out, w_out):
    r, c = lax.axis_index("row"), lax.axis_index("col")
    core = lax.rem(c, 2)
    rows = r * 32 + jnp.arange(32, dtype=jnp.int32)
    cols = c * 32 + jnp.arange(32, dtype=jnp.int32)
    valid_rows = residue_valid(rows, chain_counts, crop_skip)
    valid_cols = residue_valid(cols, chain_counts, crop_skip)
    mask = (valid_rows[:, None] * valid_cols[None, :]).reshape(1024, 1)
    pf = pair.reshape(1024, 128).astype(F32)
    ct = cotangent.reshape(1024, 128).astype(F32)
    mean = jnp.mean(pf, axis=-1, keepdims=True)
    var = jnp.mean((pf - mean) ** 2, axis=-1, keepdims=True)
    rstd = 1.0 / jnp.sqrt(var + 1e-05)
    xhat = (pf - mean) * rstd
    x = xhat.astype(BF)
    s_proj = jnp.dot(x, w_proj, preferred_element_type=F32)
    s_gate = jnp.dot(x, w_gate_in, preferred_element_type=F32)
    sig = jax.nn.sigmoid(s_gate)
    both = (mask * sig * s_proj).astype(BF)
    message = both.T.reshape(2, 128, 8, 128).transpose(1, 0, 2, 3).reshape(128, 16, 128)
    full = run(channels_kernel, message, jax.ShapeDtypeStruct((256, 16, 128), BF), 1)

    def matrix(a):
        return a.reshape(16, 16, 8, 4, 32).transpose(0, 2, 3, 1, 4).reshape(512, 512)

    def unmatrix(a):
        return a.reshape(8, 8, 4, 16, 32).transpose(0, 3, 1, 2, 4).reshape(128, 8, 128)

    left = matrix(full[:, :8])
    right = matrix(full[:, 8:])
    left_half = lax.dynamic_slice(left, (core * 256, 0), (256, 512))
    tri_half = lax.dot_general(left_half, right, (((1,), (1,)), ((), ())), preferred_element_type=F32).astype(BF)
    tri = run(cells_kernel, unmatrix(tri_half), jax.ShapeDtypeStruct((128, 8, 128), BF), 2)
    tri = tri.reshape(128, 1024).T.astype(F32)
    tmean = jnp.mean(tri, axis=-1, keepdims=True)
    tvar = jnp.mean((tri - tmean) ** 2, axis=-1, keepdims=True)
    trstd = 1.0 / jnp.sqrt(tvar + 1e-05)
    that = (tri - tmean) * trstd
    tnorm = that.astype(BF)
    gout = jax.nn.sigmoid(jnp.dot(x, w_gate_out, preferred_element_type=F32))
    y = jnp.dot(tnorm, w_out, preferred_element_type=F32)
    updated = (pf + gout * y).astype(BF)
    d_y = (ct * gout).astype(BF)
    d_sgout = (ct * y * gout * (1.0 - gout)).astype(BF)
    d_tnorm = jnp.dot(d_y, w_out.T, preferred_element_type=F32)
    d_tri = (
        trstd
        * (
            d_tnorm
            - jnp.mean(d_tnorm, axis=-1, keepdims=True)
            - that * jnp.mean(d_tnorm * that, axis=-1, keepdims=True)
        )
    ).astype(BF)
    dfull = run(channels_kernel, d_tri.T.reshape(128, 8, 128), jax.ShapeDtypeStruct((256, 8, 128), BF), 3)
    dt = matrix(dfull)
    dt_rows = lax.dynamic_slice(dt, (core * 256, 0), (256, 512))
    dt_cols = lax.dynamic_slice(dt, (0, core * 256), (512, 256))
    d_left = jnp.dot(dt_rows, right, preferred_element_type=F32).astype(BF)
    d_right = lax.dot_general(dt_cols, left, (((0,), (0,)), ((), ())), preferred_element_type=F32).astype(BF)
    back = jnp.concatenate([unmatrix(d_left), unmatrix(d_right)], axis=1)
    back = run(cells_kernel, back, jax.ShapeDtypeStruct((128, 16, 128), BF), 4)
    d_both = back.reshape(128, 2, 1024).transpose(2, 1, 0).reshape(1024, 256).astype(F32)
    d_proj = (d_both * mask * sig).astype(BF)
    d_gate = (d_both * mask * s_proj * sig * (1.0 - sig)).astype(BF)
    d_x = (
        jnp.dot(d_proj, w_proj.T, preferred_element_type=F32)
        + jnp.dot(d_gate, w_gate_in.T, preferred_element_type=F32)
        + jnp.dot(d_sgout, w_gate_out.T, preferred_element_type=F32)
    )
    d_pair = rstd * (
        d_x - jnp.mean(d_x, axis=-1, keepdims=True) - xhat * jnp.mean(d_x * xhat, axis=-1, keepdims=True)
    )
    grad_pair = (ct + d_pair).astype(BF)
    t_proj = jnp.dot(x.T, d_proj, preferred_element_type=F32)
    t_gate = jnp.dot(x.T, d_gate, preferred_element_type=F32)
    t_gout = jnp.dot(x.T, d_sgout, preferred_element_type=F32)
    t_out = jnp.dot(tnorm.T, d_y, preferred_element_type=F32)
    terms = jnp.concatenate([t_proj, t_gate, t_gout, t_out], axis=1).reshape(16, 48, 128)
    scratch = [
        pltpu.VMEM((16, 48, 128), F32), pltpu.VMEM((48, 128), F32), pltpu.VMEM((48, 128), F32),
        pltpu.VMEM((16, 48, 128), F32),
    ]
    sums = run(sum_kernel, terms, jax.ShapeDtypeStruct((16, 48, 128), F32), 5, scratch)
    sums = sums.reshape(128, 768) * (1.0 / 512)
    shape = (32, 32, 128)
    return (
        updated.reshape(shape), grad_pair.reshape(shape),
        sums[:, :256], sums[:, 256:512], sums[:, 512:640], sums[:, 640:],
    )


def solution(mesh):
    in_specs = (P("row", "col", None), P("row", "col", None), P(), P(), P(), P(), P(), P())
    out_specs = (P("row", "col", None), P("row", "col", None), P(), P(), P(), P())
    return jax.shard_map(shards, mesh=mesh, in_specs=in_specs, out_specs=out_specs, check_vma=False)
```

```python
import jax
import jax.numpy as jnp
from jax import lax
from jax.experimental import pallas as pl
from jax.experimental.pallas import tpu as pltpu
from jax.sharding import PartitionSpec as P

MESH = pl.DeviceIdType.MESH
BF = jnp.bfloat16
F32 = jnp.float32
EPS = 1e-05


def dot(a, b, dims=((1,), (0,))):
    return lax.dot_general(a, b, (dims, ((), ())), preferred_element_type=F32)


def greet(r, c):
    barrier = pltpu.get_barrier_semaphore()

    def body(s, _):
        pl.semaphore_signal(barrier, inc=1, device_id=(lax.rem(r + s, 16), c), device_id_type=MESH)
        pl.semaphore_signal(barrier, inc=1, device_id=(r, lax.rem(c + s, 16)), device_id_type=MESH)
        return 0

    lax.fori_loop(1, 16, body, 0)


def tell(r, c, sem):
    pl.semaphore_wait(pltpu.get_barrier_semaphore(), 30)

    def body(s, _):
        pl.semaphore_signal(sem, inc=1, device_id=(r, lax.rem(c + s, 16)), device_id_type=MESH)
        return 0

    lax.fori_loop(1, 16, body, 0)


def remote(src, dst, send, recv, device):
    return pltpu.make_async_remote_copy(
        src_ref=src, dst_ref=dst, send_sem=send, recv_sem=recv, device_id=device, device_id_type=MESH
    )


def arrived(buf, sem):
    pltpu.make_async_copy(buf, buf, sem).wait()


def to_channels(src, dst, send, recv, r, c):
    half, m, core = r // 8, c // 2, lax.rem(c, 2)
    r8 = lax.rem(r, 8)
    own = r * 8 + m

    @pl.when(core == half)
    def _():
        pltpu.make_async_copy(src.at[own], dst.at[r8, c], recv).start()

    @pl.when(core != half)
    def _():
        remote(src.at[own], dst.at[r8, c], send, recv, (r, m * 2 + half)).start()

    def body(s, _):
        r2 = lax.rem(r + lax.rem(s, 16), 16)
        m2 = lax.rem(m + s // 16, 8)
        remote(src.at[r2 * 8 + m2], dst.at[r8, c], send, recv, (r2, m2 * 2 + half)).start()
        return 0

    lax.fori_loop(1, 128, body, 0)


def to_cells(src, dst, send, recv, r, c):
    half, m, core = r // 8, c // 2, lax.rem(c, 2)
    r8 = lax.rem(r, 8)
    channel = r * 8 + m

    @pl.when(core == half)
    def _():
        pltpu.make_async_copy(src.at[r8, c], dst.at[channel], recv).start()

    @pl.when(core != half)
    def _():
        remote(src.at[r8, c], dst.at[channel], send, recv, (core * 8 + r8, c)).start()

    def body(s, _):
        q = lax.rem(r + lax.rem(s, 8), 8)
        c2 = lax.rem(c + s // 8, 16)
        remote(src.at[q, c2], dst.at[channel], send, recv, (core * 8 + q, c2)).start()
        return 0

    lax.fori_loop(1, 128, body, 0)


def sent(src, send, r, c):
    same = r // 8 == lax.rem(c, 2)

    @pl.when(same)
    def _():
        arrived(src.at[pl.ds(0, 127)], send)

    @pl.when(jnp.logical_not(same))
    def _():
        arrived(src, send)


def along_col(pick, dst, send, recv, r, c):
    pltpu.make_async_copy(pick(c), dst.at[c], recv).start()

    def body(s, _):
        c2 = lax.rem(c + s, 16)
        remote(pick(c2), dst.at[c], send, recv, (r, c2)).start()
        return 0

    lax.fori_loop(1, 16, body, 0)


def along_row(src, dst, send, recv, r, c):
    pltpu.make_async_copy(src, dst.at[r], recv).start()

    def body(s, _):
        remote(src, dst.at[r], send, recv, (lax.rem(r + s, 16), c)).start()
        return 0

    lax.fori_loop(1, 16, body, 0)


def valid_of(place, counts, skip):
    start = jnp.int32(0)
    valid = jnp.zeros(place.shape, F32)
    for n in range(counts.shape[0]):
        end = start + counts[n]
        inside = (place >= start) & (place < end) & (place - start >= skip[n])
        valid = jnp.where(inside, 1.0, valid)
        start = end
    return valid


def kernel(
    counts, skip, pair, cot, w_proj, w_gin, w_gout, w_out,
    upd, gpair, g_proj, g_gin, g_gout, g_out,
    wp_t, wg_t, wgo_t, wo_t, perm,
    xh, xb, rstd, pt, ctt, gate, slope, go, dgo, dtn, dyb, tnb, dsb, dpb, dgb,
    f_left, f_right, f_mat, left, right, dmat, partial, got,
    m_r, m_l, m_t, m_d, m_dl, m_dr,
    b_r, b_l, b_t, b_d, b_dl, b_dr,
    e_src, e_got, e_part, e_parts, e_tot, e_out,
    s_src, s_got, s_part, s_parts, s_tot, s_out,
    send, recv, reg,
):
    r, c = lax.axis_index("row"), lax.axis_index("col")
    core = lax.rem(c, 2)
    sibling = (r, c + 1 - 2 * core)
    greet(r, c)

    wp_t[...] = w_proj[...].astype(F32).T.astype(BF)
    wg_t[...] = w_gin[...].astype(F32).T.astype(BF)
    wgo_t[...] = w_gout[...].astype(F32).T.astype(BF)
    wo_t[...] = w_out[...].astype(F32).T.astype(BF)
    i0 = lax.broadcasted_iota(jnp.int32, (128, 128), 0)
    i1 = lax.broadcasted_iota(jnp.int32, (128, 128), 1)
    eye = jnp.where(i0 == i1, 1.0, 0.0).astype(BF)

    tell(r, c, reg.at[0])

    def forward(q, _):
        p = pair[pl.ds(q * 4, 4)].reshape(128, 128)
        p_t = dot(eye, p, ((1,), (1,)))
        pt[q] = p_t
        mean = jnp.mean(p_t, axis=0, keepdims=True)
        dev = p_t - mean
        var = jnp.mean(dev * dev, axis=0, keepdims=True)
        rs = 1.0 / jnp.sqrt(var + EPS)
        x_f = dev * rs
        x = x_f.astype(BF)
        xh[q] = x_f
        rstd[q] = jnp.broadcast_to(rs, (8, 128))
        at = pl.ds(pl.multiple_of(q * 128, 128), 128)
        xb[:, at] = x
        s = dot(wp_t[...], x)
        sig = jax.nn.sigmoid(dot(wg_t[...], x))
        lane = lax.broadcasted_iota(jnp.int32, (1, 128), 1)
        mask = valid_of(r * 32 + q * 4 + lane // 32, counts, skip) * valid_of(c * 32 + lane % 32, counts, skip)
        open_ = mask * sig
        both = open_ * s
        gate[q] = open_
        slope[q] = both * (1.0 - sig)
        f_left[pl.ds(q, 128, stride=8), :] = both[:128]
        f_right[pl.ds(q, 128, stride=8), :] = both[128:]
        return 0

    lax.fori_loop(0, 8, forward, 0)
    m_r[...] = f_right[...].reshape(128, 8, 128).astype(BF)
    pl.semaphore_wait(reg.at[0], 15)
    to_channels(m_r, b_r, send.at[0], recv.at[0], r, c)
    m_l[...] = f_left[...].reshape(128, 8, 128).astype(BF)
    to_channels(m_l, b_l, send.at[1], recv.at[1], r, c)

    j0 = lax.broadcasted_iota(jnp.int32, (512, 512), 0)
    j1 = lax.broadcasted_iota(jnp.int32, (512, 512), 1)
    swapped = (j0 % 128) // 32 * 128 + j0 // 128 * 32 + j0 % 32
    perm[...] = jnp.where(swapped == j1, 1.0, 0.0).astype(BF)

    def before(q, _):
        at = pl.ds(pl.multiple_of(q * 128, 128), 128)
        ct = dot(eye, cot[pl.ds(q * 4, 4)].reshape(128, 128), ((1,), (1,)))
        ctt[q] = ct
        g = jax.nn.sigmoid(dot(wgo_t[...], xb[:, at]))
        go[q] = g
        dy_f = ct * g
        dgo[q] = dy_f * (1.0 - g)
        dy = dy_f.astype(BF)
        dyb[:, at] = dy
        dt = dot(w_out[...], dy)
        dtn[q] = dt - jnp.mean(dt, axis=0, keepdims=True)
        return 0

    lax.fori_loop(0, 8, before, 0)

    def matrix(buf, out):
        rows = []
        for g in range(4):
            cols = [buf[:, 4 * g + n].astype(F32).reshape(64, 128).astype(BF) for n in range(4)]
            rows.append(jnp.concatenate(cols, axis=1))
        o = dot(jnp.concatenate(rows, axis=0), perm[...])
        for g in range(4):
            for a in range(4):
                f_mat[pl.ds(g * 256 + a, 64, stride=4), :] = o[g * 64:(g + 1) * 64, a * 128:(a + 1) * 128]
        for g in range(4):
            out[:, g * 128:(g + 1) * 128] = f_mat[g * 256:(g + 1) * 256].astype(BF)

    def messages(mat, out):
        for g in range(4):
            f_mat[g * 256:(g + 1) * 256] = mat[:, g * 128:(g + 1) * 128]
        rows = []
        for g in range(4):
            cols = [f_mat[pl.ds(g * 256 + a, 64, stride=4), :].astype(BF) for a in range(4)]
            rows.append(jnp.concatenate(cols, axis=1))
        o = dot(jnp.concatenate(rows, axis=0), perm[...])
        for g in range(4):
            for n in range(4):
                out[:, 4 * g + n] = o[g * 64:(g + 1) * 64, n * 128:(n + 1) * 128].reshape(8, 8, 128).astype(BF)

    arrived(b_r, recv.at[0])
    mine = right.at[pl.ds(pl.multiple_of(core * 256, 256), 256)]
    matrix(b_r, mine)
    swap = remote(mine, mine, send.at[6], recv.at[6], sibling)
    swap.start()
    arrived(b_l, recv.at[1])
    matrix(b_l, left)
    swap.wait_recv()
    messages(dot(left[...], right[...], ((1,), (1,))), m_t)
    to_cells(m_t, b_t, send.at[2], recv.at[2], r, c)
    arrived(b_t, recv.at[2])
    f_left[...] = b_t[...].astype(F32).reshape(1024, 128)

    def middle(q, _):
        at = pl.ds(pl.multiple_of(q * 128, 128), 128)
        t = f_left[pl.ds(q, 128, stride=8), :]
        dev = t - jnp.mean(t, axis=0, keepdims=True)
        rs = 1.0 / jnp.sqrt(jnp.mean(dev * dev, axis=0, keepdims=True) + EPS)
        that = dev * rs
        tnb[:, at] = that.astype(BF)
        d = dtn[q]
        f_right[pl.ds(q, 128, stride=8), :] = rs * (d - that * jnp.mean(d * that, axis=0, keepdims=True))
        return 0

    lax.fori_loop(0, 8, middle, 0)
    m_d[...] = f_right[...].reshape(128, 8, 128).astype(BF)
    to_channels(m_d, b_d, send.at[3], recv.at[3], r, c)

    def after(q, _):
        at = pl.ds(pl.multiple_of(q * 128, 128), 128)
        y = dot(wo_t[...], tnb[:, at])
        dsb[:, at] = (dgo[q] * y).astype(BF)
        u = (pt[q] + go[q] * y).astype(BF)
        upd[pl.ds(q * 4, 4)] = dot(u, eye, ((0,), (0,))).astype(BF).reshape(4, 32, 128)
        return 0

    lax.fori_loop(0, 8, after, 0)
    e_src[pl.ds(0, 8)] = dot(xb[...], dsb[...], ((1,), (1,))).reshape(8, 16, 128)
    e_src[pl.ds(8, 8)] = dot(tnb[...], dyb[...], ((1,), (1,))).reshape(8, 16, 128)
    along_col(lambda n: e_src.at[n], e_got, send.at[7], recv.at[7], r, c)

    arrived(b_d, recv.at[3])
    matrix(b_d, dmat)
    theirs = pl.ds(pl.multiple_of((1 - core) * 256, 256), 256)
    ours = pl.ds(pl.multiple_of(core * 256, 256), 256)
    partial[...] = dot(dmat[:, theirs], left[...], ((0,), (0,)))
    cross = remote(partial, got, send.at[8], recv.at[8], sibling)
    cross.start()
    messages(dot(dmat[...], right[...]), m_dl)
    to_cells(m_dl, b_dl, send.at[4], recv.at[4], r, c)
    part = dot(dmat[:, ours], left[...], ((0,), (0,)))
    cross.wait_recv()
    messages(part + got[...], m_dr)
    to_cells(m_dr, b_dr, send.at[5], recv.at[5], r, c)

    arrived(e_got, recv.at[7])
    e_part[...] = jnp.sum(e_got[...], axis=0)
    along_row(e_part, e_parts, send.at[9], recv.at[9], r, c)

    def back(lo, f):
        def body(q, _):
            at = pl.ds(pl.multiple_of(q * 128, 128), 128)
            d = f[pl.ds(q, 128, stride=8), :]
            dpb[lo:lo + 128, at] = (d * gate[q, lo:lo + 128]).astype(BF)
            dgb[lo:lo + 128, at] = (d * slope[q, lo:lo + 128]).astype(BF)
            return 0

        lax.fori_loop(0, 8, body, 0)
        n = lo // 32
        s_src[pl.ds(n, 4)] = dot(xb[...], dpb[lo:lo + 128, :], ((1,), (1,))).reshape(4, 32, 128)
        s_src[pl.ds(8 + n, 4)] = dot(xb[...], dgb[lo:lo + 128, :], ((1,), (1,))).reshape(4, 32, 128)

    arrived(b_dl, recv.at[4])
    f_left[...] = b_dl[...].astype(F32).reshape(1024, 128)
    back(0, f_left)
    arrived(b_dr, recv.at[5])
    f_right[...] = b_dr[...].astype(F32).reshape(1024, 128)
    back(128, f_right)
    along_col(lambda n: s_src.at[n], s_got, send.at[10], recv.at[10], r, c)

    arrived(e_parts, recv.at[9])
    e_tot[...] = jnp.sum(e_parts[...], axis=0)
    along_col(lambda n: e_tot, e_out, send.at[11], recv.at[11], r, c)

    arrived(s_got, recv.at[10])
    s_part[...] = jnp.sum(s_got[...], axis=0)
    along_row(s_part, s_parts, send.at[12], recv.at[12], r, c)

    def last(q, _):
        at = pl.ds(pl.multiple_of(q * 128, 128), 128)
        dx = dot(w_proj[...], dpb[:, at]) + dot(w_gin[...], dgb[:, at]) + dot(w_gout[...], dsb[:, at])
        x_f = xh[q]
        dx = dx - jnp.mean(dx, axis=0, keepdims=True) - x_f * jnp.mean(dx * x_f, axis=0, keepdims=True)
        u = (ctt[q] + rstd[q][:1] * dx).astype(BF)
        gpair[pl.ds(q * 4, 4)] = dot(u, eye, ((0,), (0,))).astype(BF).reshape(4, 32, 128)
        return 0

    lax.fori_loop(0, 8, last, 0)

    arrived(s_parts, recv.at[12])
    s_tot[...] = jnp.sum(s_parts[...], axis=0)
    along_col(lambda n: s_tot, s_out, send.at[13], recv.at[13], r, c)
    scale = 1.0 / 512
    arrived(e_out, recv.at[11])
    g_gout[...] = e_out[pl.ds(0, 8)].reshape(128, 128) * scale
    g_out[...] = e_out[pl.ds(8, 8)].reshape(128, 128) * scale
    arrived(s_out, recv.at[13])
    for lo in (0, 128):
        n = lo // 32
        g_proj[:, lo:lo + 128] = s_out[pl.ds(n, 4)].reshape(128, 128) * scale
        g_gin[:, lo:lo + 128] = s_out[pl.ds(8 + n, 4)].reshape(128, 128) * scale

    for n in range(6):
        sent(m_r, send.at[n], r, c)
    swap.wait_send()
    cross.wait_send()
    for n in (7, 9, 11):
        arrived(e_got.at[pl.ds(0, 15)], send.at[n])
    for n in (10, 12, 13):
        arrived(s_got.at[pl.ds(0, 15)], send.at[n])


def shards(pair, cotangent, chain_counts, crop_skip, w_proj, w_gate_in, w_gate_out, w_out):
    vmem = pl.BlockSpec(memory_space=pltpu.VMEM)
    smem = pl.BlockSpec(memory_space=pltpu.SMEM)
    v = pltpu.VMEM
    scratch = (
        [v((256, 128), BF), v((256, 128), BF), v((128, 128), BF), v((128, 128), BF), v((512, 512), BF)]
        + [v((8, 128, 128), F32), v((128, 1024), BF), v((8, 8, 128), F32), v((8, 128, 128), F32), v((8, 128, 128), F32)]
        + [v((8, 256, 128), F32), v((8, 256, 128), F32)]
        + [v((8, 128, 128), F32)] * 3
        + [v((128, 1024), BF)] * 3
        + [v((256, 1024), BF)] * 2
        + [v((1024, 128), F32)] * 2
        + [v((1024, 128), F32), v((256, 512), BF), v((512, 512), BF), v((256, 512), BF)]
        + [v((256, 512), F32)] * 2
        + [v((128, 8, 128), BF)] * 2 + [v((8, 16, 8, 128), BF)] + [v((128, 8, 128), BF)] + [v((8, 16, 8, 128), BF)] * 2
        + [v((8, 16, 8, 128), BF)] * 2 + [v((128, 8, 128), BF)] + [v((8, 16, 8, 128), BF)] + [v((128, 8, 128), BF)] * 2
        + [v((16, 16, 128), F32)] * 2 + [v((16, 128), F32), v((16, 16, 128), F32), v((16, 128), F32), v((16, 16, 128), F32)]
        + [v((16, 32, 128), F32)] * 2 + [v((32, 128), F32), v((16, 32, 128), F32), v((32, 128), F32), v((16, 32, 128), F32)]
        + [pltpu.SemaphoreType.DMA((14,)), pltpu.SemaphoreType.DMA((14,)), pltpu.SemaphoreType.REGULAR((1,))]
    )
    s = jax.ShapeDtypeStruct
    return pl.pallas_call(
        kernel,
        out_shape=(
            s((32, 32, 128), BF), s((32, 32, 128), BF), s((128, 256), F32), s((128, 256), F32),
            s((128, 128), F32), s((128, 128), F32),
        ),
        in_specs=[smem, smem] + [vmem] * 6,
        out_specs=(vmem,) * 6,
        scratch_shapes=scratch,
        compiler_params=pltpu.CompilerParams(collective_id=1, has_side_effects=True, vmem_limit_bytes=48 << 20),
    )(chain_counts, crop_skip, pair, cotangent, w_proj, w_gate_in, w_gate_out, w_out)


def solution(mesh):
    in_specs = (P("row", "col", None), P("row", "col", None), P(), P(), P(), P(), P(), P())
    out_specs = (P("row", "col", None), P("row", "col", None), P(), P(), P(), P())
    return jax.shard_map(shards, mesh=mesh, in_specs=in_specs, out_specs=out_specs, check_vma=False)
```

```python
import jax
import jax.numpy as jnp
from jax import lax
from jax.experimental import pallas as pl
from jax.experimental.pallas import tpu as pltpu
from jax.sharding import PartitionSpec as P

MESH = pl.DeviceIdType.MESH
BF = jnp.bfloat16
F32 = jnp.float32
EPS = 1e-05


def dot(a, b, dims=((1,), (0,))):
    return lax.dot_general(a, b, (dims, ((), ())), preferred_element_type=F32)


def greet(r, c):
    barrier = pltpu.get_barrier_semaphore()

    def body(s, _):
        pl.semaphore_signal(barrier, inc=1, device_id=(lax.rem(r + s, 16), c), device_id_type=MESH)
        pl.semaphore_signal(barrier, inc=1, device_id=(r, lax.rem(c + s, 16)), device_id_type=MESH)
        return 0

    lax.fori_loop(1, 16, body, 0)


def tell(r, c, sem):
    pl.semaphore_wait(pltpu.get_barrier_semaphore(), 30)

    def body(s, _):
        pl.semaphore_signal(sem, inc=1, device_id=(r, lax.rem(c + s, 16)), device_id_type=MESH)
        return 0

    lax.fori_loop(1, 16, body, 0)


def remote(src, dst, send, recv, device):
    return pltpu.make_async_remote_copy(
        src_ref=src, dst_ref=dst, send_sem=send, recv_sem=recv, device_id=device, device_id_type=MESH
    )


def arrived(buf, sem):
    pltpu.make_async_copy(buf, buf, sem).wait()


def far_first(u):
    y = u >> 2
    dy = jnp.where(y == 0, 2, jnp.where(y == 1, 1, jnp.where(y == 2, 3, 0)))
    return 1 - (u & 1), 1 - ((u >> 1) & 1), dy


def other_chip(m, dx, dy):
    return (((m >> 2) ^ dx) << 2) + (((m & 3) + dy) & 3)


def to_channels(src, dst, send, recv, r, c):
    half, m, core = r // 8, c // 2, lax.rem(c, 2)
    r8 = lax.rem(r, 8)
    own = r * 8 + m

    @pl.when(core == half)
    def _():
        pltpu.make_async_copy(src.at[own], dst.at[r8, c], recv).start()

    @pl.when(core != half)
    def _():
        remote(src.at[own], dst.at[r8, c], send, recv, (r, m * 2 + half)).start()

    def body(s, _):
        dxh, dxl, dy = far_first(s >> 3)
        t = s & 7
        k = (t + 1) >> 1
        z = ((r >> 1) + jnp.where((t & 1) == 1, 4 - k, 4 + k)) & 7
        r2 = z * 2 + ((r & 1) ^ dxh)
        m2 = other_chip(m, dxl, dy)
        remote(src.at[r2 * 8 + m2], dst.at[r8, c], send, recv, (r2, m2 * 2 + half)).start()
        return 0

    lax.fori_loop(0, 127, body, 0)


def to_cells(src, dst, send, recv, r, c):
    half, m, core = r // 8, c // 2, lax.rem(c, 2)
    r8 = lax.rem(r, 8)
    channel = r * 8 + m

    @pl.when(core == half)
    def _():
        pltpu.make_async_copy(src.at[r8, c], dst.at[channel], recv).start()

    @pl.when(core != half)
    def _():
        remote(src.at[r8, c], dst.at[channel], send, recv, (core * 8 + r8, c)).start()

    def body(s, _):
        dxh, dxl, dy = far_first(s >> 3)
        z = ((r >> 1) + 1 + s) & 3
        q = z * 2 + ((r & 1) ^ dxh)
        c2 = other_chip(m, dxl, dy) * 2 + (core ^ 1 ^ ((s >> 2) & 1))
        remote(src.at[q, c2], dst.at[channel], send, recv, (core * 8 + q, c2)).start()
        return 0

    lax.fori_loop(0, 127, body, 0)


def sent(src, send, r, c):
    same = r // 8 == lax.rem(c, 2)

    @pl.when(same)
    def _():
        arrived(src.at[pl.ds(0, 127)], send)

    @pl.when(jnp.logical_not(same))
    def _():
        arrived(src, send)


def along_col(pick, dst, send, recv, r, c):
    pltpu.make_async_copy(pick(c), dst.at[c], recv).start()

    def body(s, _):
        c2 = lax.rem(c + s, 16)
        remote(pick(c2), dst.at[c], send, recv, (r, c2)).start()
        return 0

    lax.fori_loop(1, 16, body, 0)


def along_row(src, dst, send, recv, r, c):
    pltpu.make_async_copy(src, dst.at[r], recv).start()

    def body(s, _):
        remote(src, dst.at[r], send, recv, (lax.rem(r + s, 16), c)).start()
        return 0

    lax.fori_loop(1, 16, body, 0)


def valid_of(place, counts, skip):
    start = jnp.int32(0)
    valid = jnp.zeros(place.shape, F32)
    for n in range(counts.shape[0]):
        end = start + counts[n]
        inside = (place >= start) & (place < end) & (place - start >= skip[n])
        valid = jnp.where(inside, 1.0, valid)
        start = end
    return valid


def kernel(
    counts_h, skip_h, pair_h, cot_h, w_proj_h, w_gin_h, w_gout_h, w_out_h,
    upd_h, gpair_h, sums_h,
    counts, skip, pair, cot, w_proj, w_gin, w_gout, w_out, upd, gpair,
    wp_t, wg_t, wgo_t, wo_t, perm,
    xh, xb, rstd, pt, ctt, gate, slope, go, dgo, dtn, dyb, tnb, dsb, dpb, dgb,
    f_left, f_right, f_mat, left, right, dmat, partial, got,
    m_r, m_l, m_t, m_d, m_dl, m_dr,
    b_r, b_l, b_t, b_d, b_dl, b_dr,
    s_src, s_got, s_part, s_parts, s_tot, s_out,
    send, recv, load, reg,
):
    pending = []

    r, c = lax.axis_index("row"), lax.axis_index("col")
    core = lax.rem(c, 2)
    sibling = (r, c + 1 - 2 * core)
    greet(r, c)
    loads = [
        pltpu.make_async_copy(a, b, load.at[n])
        for n, (a, b) in enumerate([
            (pair_h, pair), (w_proj_h, w_proj), (w_gin_h, w_gin), (counts_h, counts), (skip_h, skip),
            (cot_h, cot), (w_gout_h, w_gout), (w_out_h, w_out),
        ])
    ]
    for copy in loads:
        copy.start()
    i0 = lax.broadcasted_iota(jnp.int32, (128, 128), 0)
    i1 = lax.broadcasted_iota(jnp.int32, (128, 128), 1)
    eye = jnp.where(i0 == i1, 1.0, 0.0).astype(BF)
    for copy in loads[:5]:
        copy.wait()
    wp_t[...] = w_proj[...].astype(F32).T.astype(BF)
    wg_t[...] = w_gin[...].astype(F32).T.astype(BF)
    tell(r, c, reg.at[0])

    def normed(q, _):
        p = pair[pl.ds(q * 4, 4)].reshape(128, 128)
        p_t = dot(eye, p, ((1,), (1,)))
        pt[q] = p_t
        mean = jnp.mean(p_t, axis=0, keepdims=True)
        dev = p_t - mean
        var = jnp.mean(dev * dev, axis=0, keepdims=True)
        rs = 1.0 / jnp.sqrt(var + EPS)
        x_f = dev * rs
        xh[q] = x_f
        rstd[q] = jnp.broadcast_to(rs, (8, 128))
        xb[:, pl.ds(pl.multiple_of(q * 128, 128), 128)] = x_f.astype(BF)
        return 0

    def project(lo, f):
        def body(q, _):
            x = xb[:, pl.ds(pl.multiple_of(q * 128, 128), 128)]
            s = dot(wp_t[lo:lo + 128, :], x)
            sig = jax.nn.sigmoid(dot(wg_t[lo:lo + 128, :], x))
            lane = lax.broadcasted_iota(jnp.int32, (1, 128), 1)
            mask = valid_of(r * 32 + q * 4 + lane // 32, counts, skip) * valid_of(c * 32 + lane % 32, counts, skip)
            open_ = mask * sig
            both = open_ * s
            gate[q, lo:lo + 128] = open_
            slope[q, lo:lo + 128] = both * (1.0 - sig)
            f[pl.ds(q, 128, stride=8), :] = both
            return 0

        lax.fori_loop(0, 8, body, 0)

    lax.fori_loop(0, 8, normed, 0)
    project(128, f_right)
    m_r[...] = f_right[...].reshape(128, 8, 128).astype(BF)
    pl.semaphore_wait(reg.at[0], 15)
    to_channels(m_r, b_r, send.at[0], recv.at[0], r, c)
    pending.append(lambda: sent(m_r, send.at[0], r, c))
    project(0, f_left)
    m_l[...] = f_left[...].reshape(128, 8, 128).astype(BF)
    to_channels(m_l, b_l, send.at[1], recv.at[1], r, c)
    pending.append(lambda: sent(m_r, send.at[1], r, c))

    j0 = lax.broadcasted_iota(jnp.int32, (512, 512), 0)
    j1 = lax.broadcasted_iota(jnp.int32, (512, 512), 1)
    swapped = (j0 % 128) // 32 * 128 + j0 // 128 * 32 + j0 % 32
    perm[...] = jnp.where(swapped == j1, 1.0, 0.0).astype(BF)
    for copy in loads[5:]:
        copy.wait()
    wgo_t[...] = w_gout[...].astype(F32).T.astype(BF)
    wo_t[...] = w_out[...].astype(F32).T.astype(BF)

    def before(q, _):
        at = pl.ds(pl.multiple_of(q * 128, 128), 128)
        ct = dot(eye, cot[pl.ds(q * 4, 4)].reshape(128, 128), ((1,), (1,)))
        ctt[q] = ct
        g = jax.nn.sigmoid(dot(wgo_t[...], xb[:, at]))
        go[q] = g
        dy_f = ct * g
        dgo[q] = dy_f * (1.0 - g)
        dy = dy_f.astype(BF)
        dyb[:, at] = dy
        dt = dot(w_out[...], dy)
        dtn[q] = dt - jnp.mean(dt, axis=0, keepdims=True)
        return 0

    lax.fori_loop(0, 8, before, 0)

    def matrix(buf, out):
        rows = []
        for g in range(4):
            cols = [buf[:, 4 * g + n].astype(F32).reshape(64, 128).astype(BF) for n in range(4)]
            rows.append(jnp.concatenate(cols, axis=1))
        o = dot(jnp.concatenate(rows, axis=0), perm[...])
        for g in range(4):
            for a in range(4):
                f_mat[pl.ds(g * 256 + a, 64, stride=4), :] = o[g * 64:(g + 1) * 64, a * 128:(a + 1) * 128]
        for g in range(4):
            out[:, g * 128:(g + 1) * 128] = f_mat[g * 256:(g + 1) * 256].astype(BF)

    def messages(mat, out):
        for g in range(4):
            f_mat[g * 256:(g + 1) * 256] = mat[:, g * 128:(g + 1) * 128]
        rows = []
        for g in range(4):
            cols = [f_mat[pl.ds(g * 256 + a, 64, stride=4), :].astype(BF) for a in range(4)]
            rows.append(jnp.concatenate(cols, axis=1))
        o = dot(jnp.concatenate(rows, axis=0), perm[...])
        for g in range(4):
            for n in range(4):
                out[:, 4 * g + n] = o[g * 64:(g + 1) * 64, n * 128:(n + 1) * 128].reshape(8, 8, 128).astype(BF)

    def scatter(n):
        along_col(lambda k: s_src.at[n, k], s_got.at[n], send.at[8 + n], recv.at[8 + n], r, c)
        pending.append(lambda: arrived(s_got.at[n, pl.ds(0, 15)], send.at[8 + n]))

    def share(n):
        arrived(s_got.at[n], recv.at[8 + n])
        s_part[n] = jnp.sum(s_got[n], axis=0).astype(BF)
        along_row(s_part.at[n], s_parts.at[n], send.at[11 + n], recv.at[11 + n], r, c)
        pending.append(lambda: arrived(s_parts.at[n, pl.ds(0, 15)], send.at[11 + n]))

    def gather(n):
        arrived(s_parts.at[n], recv.at[11 + n])
        s_tot[n] = jnp.sum(s_parts[n].astype(F32), axis=0) * (1.0 / 512)
        along_col(lambda k: s_tot.at[n], s_out.at[n], send.at[14 + n], recv.at[14 + n], r, c)
        pending.append(lambda: arrived(s_got.at[n, pl.ds(0, 15)], send.at[14 + n]))

    outs = []

    def put(src, dst, n):
        copy = pltpu.make_async_copy(src, dst, load.at[8 + n])
        copy.start()
        outs.append(copy)

    mine = right.at[pl.ds(pl.multiple_of(core * 256, 256), 256)]
    arrived(b_r, recv.at[0])
    matrix(b_r, mine)
    swap = remote(mine, mine, send.at[6], recv.at[6], sibling)
    swap.start()
    pending.append(swap.wait_send)
    arrived(b_l, recv.at[1])
    matrix(b_l, left)
    swap.wait_recv()
    messages(dot(left[...], right[...], ((1,), (1,))), m_t)
    to_cells(m_t, b_t, send.at[2], recv.at[2], r, c)
    pending.append(lambda: sent(m_r, send.at[2], r, c))
    arrived(b_t, recv.at[2])
    f_left[...] = b_t[...].astype(F32).reshape(1024, 128)

    def middle(q, _):
        at = pl.ds(pl.multiple_of(q * 128, 128), 128)
        t = f_left[pl.ds(q, 128, stride=8), :]
        dev = t - jnp.mean(t, axis=0, keepdims=True)
        rs = 1.0 / jnp.sqrt(jnp.mean(dev * dev, axis=0, keepdims=True) + EPS)
        that = dev * rs
        tnb[:, at] = that.astype(BF)
        d = dtn[q]
        f_right[pl.ds(q, 128, stride=8), :] = rs * (d - that * jnp.mean(d * that, axis=0, keepdims=True))
        return 0

    lax.fori_loop(0, 8, middle, 0)
    m_d[...] = f_right[...].reshape(128, 8, 128).astype(BF)
    to_channels(m_d, b_d, send.at[3], recv.at[3], r, c)
    pending.append(lambda: sent(m_r, send.at[3], r, c))

    def after(q, _):
        at = pl.ds(pl.multiple_of(q * 128, 128), 128)
        y = dot(wo_t[...], tnb[:, at])
        dsb[:, at] = (dgo[q] * y).astype(BF)
        u = (pt[q] + go[q] * y).astype(BF)
        upd[pl.ds(q * 4, 4)] = dot(u, eye, ((0,), (0,))).astype(BF).reshape(4, 32, 128)
        return 0

    lax.fori_loop(0, 8, after, 0)
    put(upd, upd_h, 0)
    s_src[0, pl.ds(0, 8)] = dot(xb[...], dsb[...], ((1,), (1,))).reshape(8, 16, 128)
    s_src[0, pl.ds(8, 8)] = dot(tnb[...], dyb[...], ((1,), (1,))).reshape(8, 16, 128)
    scatter(0)

    arrived(b_d, recv.at[3])
    matrix(b_d, dmat)
    theirs = pl.ds(pl.multiple_of((1 - core) * 256, 256), 256)
    ours = pl.ds(pl.multiple_of(core * 256, 256), 256)
    partial[...] = dot(dmat[:, theirs], left[...], ((0,), (0,)))
    cross = remote(partial, got, send.at[7], recv.at[7], sibling)
    cross.start()
    pending.append(cross.wait_send)
    messages(dot(dmat[...], right[...]), m_dl)
    to_cells(m_dl, b_dl, send.at[4], recv.at[4], r, c)
    pending.append(lambda: sent(m_r, send.at[4], r, c))
    part = dot(dmat[:, ours], left[...], ((0,), (0,)))
    cross.wait_recv()
    messages(part + got[...], m_dr)
    to_cells(m_dr, b_dr, send.at[5], recv.at[5], r, c)
    pending.append(lambda: sent(m_r, send.at[5], r, c))
    share(0)

    def back(n, lo, f):
        def body(q, _):
            at = pl.ds(pl.multiple_of(q * 128, 128), 128)
            d = f[pl.ds(q, 128, stride=8), :]
            dpb[lo:lo + 128, at] = (d * gate[q, lo:lo + 128]).astype(BF)
            dgb[lo:lo + 128, at] = (d * slope[q, lo:lo + 128]).astype(BF)
            return 0

        lax.fori_loop(0, 8, body, 0)
        s_src[n, pl.ds(0, 8)] = dot(xb[...], dpb[lo:lo + 128, :], ((1,), (1,))).reshape(8, 16, 128)
        s_src[n, pl.ds(8, 8)] = dot(xb[...], dgb[lo:lo + 128, :], ((1,), (1,))).reshape(8, 16, 128)
        scatter(n)

    arrived(b_dl, recv.at[4])
    f_left[...] = b_dl[...].astype(F32).reshape(1024, 128)
    back(1, 0, f_left)
    gather(0)
    share(1)
    arrived(b_dr, recv.at[5])
    f_right[...] = b_dr[...].astype(F32).reshape(1024, 128)
    back(2, 128, f_right)
    gather(1)

    def last(q, _):
        at = pl.ds(pl.multiple_of(q * 128, 128), 128)
        dx = dot(w_proj[...], dpb[:, at]) + dot(w_gin[...], dgb[:, at]) + dot(w_gout[...], dsb[:, at])
        x_f = xh[q]
        dx = dx - jnp.mean(dx, axis=0, keepdims=True) - x_f * jnp.mean(dx * x_f, axis=0, keepdims=True)
        u = (ctt[q] + rstd[q][:1] * dx).astype(BF)
        gpair[pl.ds(q * 4, 4)] = dot(u, eye, ((0,), (0,))).astype(BF).reshape(4, 32, 128)
        return 0

    lax.fori_loop(0, 4, last, 0)
    share(2)
    lax.fori_loop(4, 8, last, 0)
    put(gpair, gpair_h, 1)
    for n in range(2):
        arrived(s_out.at[n], recv.at[14 + n])
        put(s_out.at[n], sums_h.at[n], 2 + n)
    gather(2)
    for wait in pending:
        wait()
    arrived(s_out.at[2], recv.at[16])
    put(s_out.at[2], sums_h.at[2], 4)
    for copy in outs:
        copy.wait()


def finish(upd, gpair, sums, upd_o, gpair_o, g_proj, g_gin, g_gout, g_out, upd_v, gpair_v, sums_v, sem):
    loads = [
        pltpu.make_async_copy(a, b, sem.at[n])
        for n, (a, b) in enumerate([(upd, upd_v), (gpair, gpair_v), (sums, sums_v)])
    ]
    for copy in loads:
        copy.start()
    flat = sums_v.reshape(6, 128, 128)
    left, right = pl.ds(0, 128), pl.ds(128, 128)
    pairs = [
        (upd_v, upd_o), (gpair_v, gpair_o), (flat.at[0], g_gout), (flat.at[1], g_out),
        (flat.at[2], g_proj.at[:, left]), (flat.at[3], g_gin.at[:, left]),
        (flat.at[4], g_proj.at[:, right]), (flat.at[5], g_gin.at[:, right]),
    ]
    stores = [pltpu.make_async_copy(a, b, sem.at[3 + n]) for n, (a, b) in enumerate(pairs)]
    for n, copy in enumerate(stores):
        if n < 3:
            loads[n].wait()
        copy.start()
    for copy in stores:
        copy.wait()


def shards(pair, cotangent, chain_counts, crop_skip, w_proj, w_gate_in, w_gate_out, w_out):
    hbm = pl.BlockSpec(memory_space=pl.ANY)
    v = pltpu.VMEM
    s = jax.ShapeDtypeStruct
    scratch = (
        [pltpu.SMEM((4,), jnp.int32)] * 2 + [v((32, 32, 128), BF)] * 2
        + [v((128, 256), BF)] * 2 + [v((128, 128), BF)] * 2 + [v((32, 32, 128), BF)] * 2
        + [v((256, 128), BF), v((256, 128), BF), v((128, 128), BF), v((128, 128), BF), v((512, 512), BF)]
        + [v((8, 128, 128), F32), v((128, 1024), BF), v((8, 8, 128), F32), v((8, 128, 128), F32), v((8, 128, 128), F32)]
        + [v((8, 256, 128), F32), v((8, 256, 128), F32)]
        + [v((8, 128, 128), F32)] * 3
        + [v((128, 1024), BF)] * 3
        + [v((256, 1024), BF)] * 2
        + [v((1024, 128), F32)] * 2
        + [v((1024, 128), F32), v((256, 512), BF), v((512, 512), BF), v((256, 512), BF)]
        + [v((256, 512), F32)] * 2
        + [v((128, 8, 128), BF)] * 2 + [v((8, 16, 8, 128), BF)] + [v((128, 8, 128), BF)] + [v((8, 16, 8, 128), BF)] * 2
        + [v((8, 16, 8, 128), BF)] * 2 + [v((128, 8, 128), BF)] + [v((8, 16, 8, 128), BF)] + [v((128, 8, 128), BF)] * 2
        + [v((3, 16, 16, 128), F32)] * 2 + [v((3, 16, 128), BF), v((3, 16, 16, 128), BF), v((3, 16, 128), F32)]
        + [v((3, 16, 16, 128), F32)]
        + [pltpu.SemaphoreType.DMA((17,)), pltpu.SemaphoreType.DMA((17,)), pltpu.SemaphoreType.DMA((13,))]
        + [pltpu.SemaphoreType.REGULAR((1,))]
    )
    block = s((32, 32, 128), BF)
    wide, square = s((128, 256), F32), s((128, 128), F32)
    results = pl.pallas_call(
        kernel,
        out_shape=(block, block, s((3, 16, 16, 128), F32)),
        in_specs=[hbm] * 8,
        out_specs=(hbm,) * 3,
        scratch_shapes=scratch,
        compiler_params=pltpu.CompilerParams(collective_id=1, has_side_effects=True, vmem_limit_bytes=60 << 20),
    )(chain_counts, crop_skip, pair, cotangent, w_proj, w_gate_in, w_gate_out, w_out)
    return pl.pallas_call(
        finish,
        out_shape=(block, block, wide, wide, square, square),
        in_specs=[hbm] * 3,
        out_specs=(hbm,) * 6,
        scratch_shapes=[v(block.shape, BF)] * 2 + [v((3, 16, 16, 128), F32), pltpu.SemaphoreType.DMA((11,))],
        compiler_params=pltpu.CompilerParams(vmem_limit_bytes=60 << 20),
    )(*results)


def solution(mesh):
    in_specs = (P("row", "col", None), P("row", "col", None), P(), P(), P(), P(), P(), P())
    out_specs = (P("row", "col", None), P("row", "col", None), P(), P(), P(), P())
    return jax.shard_map(shards, mesh=mesh, in_specs=in_specs, out_specs=out_specs, check_vma=False)
```

```python
import jax
import jax.numpy as jnp
from jax import lax
from jax.experimental import pallas as pl
from jax.experimental.pallas import tpu as pltpu
from jax.sharding import PartitionSpec as P

MESH = pl.DeviceIdType.MESH
BF = jnp.bfloat16
F32 = jnp.float32
EPS = 1e-05


def dot(a, b, dims=((1,), (0,))):
    return lax.dot_general(a, b, (dims, ((), ())), preferred_element_type=F32)


def greet(r, c):
    barrier = pltpu.get_barrier_semaphore()

    def body(s, _):
        pl.semaphore_signal(barrier, inc=1, device_id=(lax.rem(r + s, 16), c), device_id_type=MESH)
        pl.semaphore_signal(barrier, inc=1, device_id=(r, lax.rem(c + s, 16)), device_id_type=MESH)
        return 0

    lax.fori_loop(1, 16, body, 0)


def tell(r, c, sem):
    pl.semaphore_wait(pltpu.get_barrier_semaphore(), 30)

    def body(s, _):
        pl.semaphore_signal(sem, inc=1, device_id=(r, lax.rem(c + s, 16)), device_id_type=MESH)
        return 0

    lax.fori_loop(1, 16, body, 0)


def remote(src, dst, send, recv, device):
    return pltpu.make_async_remote_copy(
        src_ref=src, dst_ref=dst, send_sem=send, recv_sem=recv, device_id=device, device_id_type=MESH
    )


def arrived(buf, sem):
    pltpu.make_async_copy(buf, buf, sem).wait()


def far_first(u):
    y = u >> 2
    dy = jnp.where(y == 0, 2, jnp.where(y == 1, 1, jnp.where(y == 2, 3, 0)))
    return 1 - (u & 1), 1 - ((u >> 1) & 1), dy


def other_chip(m, dx, dy):
    return (((m >> 2) ^ dx) << 2) + (((m & 3) + dy) & 3)


def to_channels(src, dst, send, recv, r, c):
    half, m, core = r // 8, c // 2, lax.rem(c, 2)
    r8 = lax.rem(r, 8)
    own = r * 8 + m

    @pl.when(core == half)
    def _():
        pltpu.make_async_copy(src.at[own], dst.at[r8, c], recv).start()

    @pl.when(core != half)
    def _():
        remote(src.at[own], dst.at[r8, c], send, recv, (r, m * 2 + half)).start()

    def body(s, _):
        dxh, dxl, dy = far_first(s >> 3)
        t = s & 7
        k = (t + 1) >> 1
        z = ((r >> 1) + jnp.where((t & 1) == 1, 4 - k, 4 + k)) & 7
        r2 = z * 2 + ((r & 1) ^ dxh)
        m2 = other_chip(m, dxl, dy)
        remote(src.at[r2 * 8 + m2], dst.at[r8, c], send, recv, (r2, m2 * 2 + half)).start()
        return 0

    lax.fori_loop(0, 127, body, 0)


def to_cells(src, dst, send, recv, r, c):
    half, m, core = r // 8, c // 2, lax.rem(c, 2)
    r8 = lax.rem(r, 8)
    channel = r * 8 + m

    @pl.when(core == half)
    def _():
        pltpu.make_async_copy(src.at[r8, c], dst.at[channel], recv).start()

    @pl.when(core != half)
    def _():
        remote(src.at[r8, c], dst.at[channel], send, recv, (core * 8 + r8, c)).start()

    def body(s, _):
        dxh, dxl, dy = far_first(s >> 3)
        z = ((r >> 1) + 1 + s) & 3
        q = z * 2 + ((r & 1) ^ dxh)
        c2 = other_chip(m, dxl, dy) * 2 + (core ^ 1 ^ ((s >> 2) & 1))
        remote(src.at[q, c2], dst.at[channel], send, recv, (core * 8 + q, c2)).start()
        return 0

    lax.fori_loop(0, 127, body, 0)


def sent(src, send, r, c):
    same = r // 8 == lax.rem(c, 2)

    @pl.when(same)
    def _():
        arrived(src.at[pl.ds(0, 127)], send)

    @pl.when(jnp.logical_not(same))
    def _():
        arrived(src, send)


def along_col(pick, dst, send, recv, r, c):
    pltpu.make_async_copy(pick(c), dst.at[c], recv).start()

    def body(s, _):
        c2 = lax.rem(c + s, 16)
        remote(pick(c2), dst.at[c], send, recv, (r, c2)).start()
        return 0

    lax.fori_loop(1, 16, body, 0)


def along_row(src, dst, send, recv, r, c):
    pltpu.make_async_copy(src, dst.at[r], recv).start()

    def body(s, _):
        remote(src, dst.at[r], send, recv, (lax.rem(r + s, 16), c)).start()
        return 0

    lax.fori_loop(1, 16, body, 0)


def valid_of(place, counts, skip):
    start = jnp.int32(0)
    valid = jnp.zeros(place.shape, F32)
    for n in range(counts.shape[0]):
        end = start + counts[n]
        inside = (place >= start) & (place < end) & (place - start >= skip[n])
        valid = jnp.where(inside, 1.0, valid)
        start = end
    return valid


def kernel(
    counts_h, skip_h, pair_h, cot_h, w_proj_h, w_gin_h, w_gout_h, w_out_h,
    upd_h, gpair_h, sums_h,
    counts, skip, pair, cot, w_proj, w_gin, w_gout, w_out, upd, gpair,
    wp_t, wg_t, wgo_t, wo_t, perm,
    xh, xb, rstd, pt, ctt, gate, slope, go, dgo, dtn, dyb, tnb, dsb, dpb, dgb,
    f_left, f_right, f_mat, left, right, dmat, partial, got,
    m_r, m_l, m_t, m_d, m_dl, m_dr,
    b_r, b_l, b_t, b_d, b_dl, b_dr,
    s_src, s_got, s_part, s_parts, s_tot, s_out, s_sum,
    send, recv, load, reg,
):
    pending = []

    r, c = lax.axis_index("row"), lax.axis_index("col")
    core = lax.rem(c, 2)
    sibling = (r, c + 1 - 2 * core)
    greet(r, c)
    loads = [
        pltpu.make_async_copy(a, b, load.at[n])
        for n, (a, b) in enumerate([
            (pair_h, pair), (w_proj_h, w_proj), (w_gin_h, w_gin), (counts_h, counts), (skip_h, skip),
            (cot_h, cot), (w_gout_h, w_gout), (w_out_h, w_out),
        ])
    ]
    for copy in loads:
        copy.start()
    i0 = lax.broadcasted_iota(jnp.int32, (128, 128), 0)
    i1 = lax.broadcasted_iota(jnp.int32, (128, 128), 1)
    eye = jnp.where(i0 == i1, 1.0, 0.0).astype(BF)
    j0 = lax.broadcasted_iota(jnp.int32, (512, 512), 0)
    j1 = lax.broadcasted_iota(jnp.int32, (512, 512), 1)
    swapped = ((j0 >> 5) & 3) * 128 + (j0 >> 7) * 32 + (j0 & 31)
    perm[...] = jnp.where(swapped == j1, 1.0, 0.0).astype(BF)
    for copy in loads[:5]:
        copy.wait()
    wp_t[...] = w_proj[...].astype(F32).T.astype(BF)
    wg_t[...] = w_gin[...].astype(F32).T.astype(BF)
    tell(r, c, reg.at[0])

    def normed(q, _):
        p = pair[pl.ds(q * 4, 4)].reshape(128, 128)
        p_t = dot(eye, p, ((1,), (1,)))
        pt[q] = p_t
        mean = jnp.mean(p_t, axis=0, keepdims=True)
        dev = p_t - mean
        var = jnp.mean(dev * dev, axis=0, keepdims=True)
        rs = 1.0 / jnp.sqrt(var + EPS)
        x_f = dev * rs
        xh[q] = x_f
        rstd[q] = jnp.broadcast_to(rs, (8, 128))
        xb[:, pl.ds(pl.multiple_of(q * 128, 128), 128)] = x_f.astype(BF)
        return 0

    def project(lo, f):
        def body(q, _):
            x = xb[:, pl.ds(pl.multiple_of(q * 128, 128), 128)]
            s = dot(wp_t[lo:lo + 128, :], x)
            sig = jax.nn.sigmoid(dot(wg_t[lo:lo + 128, :], x))
            lane = lax.broadcasted_iota(jnp.int32, (1, 128), 1)
            mask = valid_of(r * 32 + q * 4 + lane // 32, counts, skip) * valid_of(c * 32 + lane % 32, counts, skip)
            open_ = mask * sig
            both = open_ * s
            gate[q, lo:lo + 128] = open_
            slope[q, lo:lo + 128] = both * (1.0 - sig)
            f[pl.ds(q, 128, stride=8), :] = both
            return 0

        lax.fori_loop(0, 8, body, 0, unroll=4)

    lax.fori_loop(0, 8, normed, 0, unroll=4)
    project(128, f_right)
    m_r[...] = f_right[...].reshape(128, 8, 128).astype(BF)
    pl.semaphore_wait(reg.at[0], 15)
    to_channels(m_r, b_r, send.at[0], recv.at[0], r, c)
    pending.append(lambda: sent(m_r, send.at[0], r, c))
    project(0, f_left)
    m_l[...] = f_left[...].reshape(128, 8, 128).astype(BF)
    to_channels(m_l, b_l, send.at[1], recv.at[1], r, c)
    pending.append(lambda: sent(m_r, send.at[1], r, c))

    def before(q, _):
        at = pl.ds(pl.multiple_of(q * 128, 128), 128)
        ct = dot(eye, cot[pl.ds(q * 4, 4)].reshape(128, 128), ((1,), (1,)))
        ctt[q] = ct
        g = jax.nn.sigmoid(dot(wgo_t[...], xb[:, at]))
        go[q] = g
        dy_f = ct * g
        dgo[q] = dy_f * (1.0 - g)
        dy = dy_f.astype(BF)
        dyb[:, at] = dy
        dt = dot(w_out[...], dy)
        dtn[q] = dt - jnp.mean(dt, axis=0, keepdims=True)
        return 0


    def turned(buf):
        rows = []
        for g in range(4):
            cols = [buf[:, 4 * g + n].astype(F32).reshape(64, 128).astype(BF) for n in range(4)]
            rows.append(jnp.concatenate(cols, axis=1))
        return dot(jnp.concatenate(rows, axis=0), perm[...])

    def natural(buf, out):
        o = turned(buf)
        for g in range(4):
            for a in range(4):
                f_mat[pl.ds(g * 256 + a, 64, stride=4), :] = o[g * 64:(g + 1) * 64, a * 128:(a + 1) * 128]
        for g in range(4):
            out[:, g * 128:(g + 1) * 128] = f_mat[g * 256:(g + 1) * 256].astype(BF)

    def matrix(buf, out):
        o = turned(buf)
        for g in range(4):
            for a in range(4):
                out[a * 64:(a + 1) * 64, g * 128:(g + 1) * 128] = o[g * 64:(g + 1) * 64, a * 128:(a + 1) * 128].astype(BF)

    def spread(block, out):
        rows = [jnp.concatenate([block(a, g).astype(BF) for a in range(4)], axis=1) for g in range(4)]
        o = dot(jnp.concatenate(rows, axis=0), perm[...])
        for g in range(4):
            for n in range(4):
                out[:, 4 * g + n] = o[g * 64:(g + 1) * 64, n * 128:(n + 1) * 128].reshape(8, 8, 128).astype(BF)

    def messages(mat, out):
        spread(lambda a, g: mat[a * 64:(a + 1) * 64, g * 128:(g + 1) * 128], out)

    def natural_messages(mat, out):
        for g in range(4):
            f_mat[g * 256:(g + 1) * 256] = mat[:, g * 128:(g + 1) * 128]
        spread(lambda a, g: f_mat[pl.ds(g * 256 + a, 64, stride=4), :], out)

    def scatter(n):
        along_col(lambda k: s_src.at[n, k], s_got.at[n], send.at[8 + n], recv.at[8 + n], r, c)
        pending.append(lambda: arrived(s_got.at[n, pl.ds(0, 15)], send.at[8 + n]))

    def share(n):
        arrived(s_got.at[n], recv.at[8 + n])
        s_part[n] = jnp.sum(s_got[n].astype(F32), axis=0).astype(BF)
        along_row(s_part.at[n], s_parts.at[n], send.at[11 + n], recv.at[11 + n], r, c)
        pending.append(lambda: arrived(s_parts.at[n, pl.ds(0, 15)], send.at[11 + n]))

    def gather(n):
        arrived(s_parts.at[n], recv.at[11 + n])
        s_tot[n] = (jnp.sum(s_parts[n].astype(F32), axis=0) * (1.0 / 512)).astype(BF)
        along_col(lambda k: s_tot.at[n], s_out.at[n], send.at[14 + n], recv.at[14 + n], r, c)
        pending.append(lambda: arrived(s_got.at[n, pl.ds(0, 15)], send.at[14 + n]))

    outs = []

    def put(src, dst, n):
        copy = pltpu.make_async_copy(src, dst, load.at[8 + n])
        copy.start()
        outs.append(copy)

    mine = right.at[pl.ds(pl.multiple_of(core * 256, 256), 256)]
    arrived(b_r, recv.at[0])
    natural(b_r, mine)
    swap = remote(mine, mine, send.at[6], recv.at[6], sibling)
    swap.start()
    pending.append(swap.wait_send)

    for copy in loads[5:]:
        copy.wait()
    wgo_t[...] = w_gout[...].astype(F32).T.astype(BF)
    wo_t[...] = w_out[...].astype(F32).T.astype(BF)
    lax.fori_loop(0, 8, before, 0, unroll=2)
    arrived(b_l, recv.at[1])
    matrix(b_l, left)
    swap.wait_recv()
    messages(dot(left[...], right[...], ((1,), (1,))), m_t)
    to_cells(m_t, b_t, send.at[2], recv.at[2], r, c)
    pending.append(lambda: sent(m_r, send.at[2], r, c))
    arrived(b_t, recv.at[2])
    f_left[...] = b_t[...].astype(F32).reshape(1024, 128)

    def middle(q, _):
        at = pl.ds(pl.multiple_of(q * 128, 128), 128)
        t = f_left[pl.ds(q, 128, stride=8), :]
        dev = t - jnp.mean(t, axis=0, keepdims=True)
        rs = 1.0 / jnp.sqrt(jnp.mean(dev * dev, axis=0, keepdims=True) + EPS)
        that = dev * rs
        tnb[:, at] = that.astype(BF)
        d = dtn[q]
        f_right[pl.ds(q, 128, stride=8), :] = rs * (d - that * jnp.mean(d * that, axis=0, keepdims=True))
        return 0

    lax.fori_loop(0, 8, middle, 0, unroll=4)
    m_d[...] = f_right[...].reshape(128, 8, 128).astype(BF)
    to_channels(m_d, b_d, send.at[3], recv.at[3], r, c)
    pending.append(lambda: sent(m_r, send.at[3], r, c))

    def after(q, _):
        at = pl.ds(pl.multiple_of(q * 128, 128), 128)
        y = dot(wo_t[...], tnb[:, at])
        dsb[:, at] = (dgo[q] * y).astype(BF)
        u = (pt[q] + go[q] * y).astype(BF)
        upd[pl.ds(q * 4, 4)] = dot(u, eye, ((0,), (0,))).astype(BF).reshape(4, 32, 128)
        return 0

    lax.fori_loop(0, 8, after, 0, unroll=2)
    put(upd, upd_h, 0)
    s_src[0, pl.ds(0, 8)] = dot(xb[...], dsb[...], ((1,), (1,))).reshape(8, 16, 128).astype(BF)
    s_src[0, pl.ds(8, 8)] = dot(tnb[...], dyb[...], ((1,), (1,))).reshape(8, 16, 128).astype(BF)
    scatter(0)

    arrived(b_d, recv.at[3])
    matrix(b_d, dmat)
    theirs = pl.ds(pl.multiple_of((1 - core) * 256, 256), 256)
    ours = pl.ds(pl.multiple_of(core * 256, 256), 256)
    partial[...] = dot(dmat[:, theirs], left[...], ((0,), (0,))).astype(BF)
    cross = remote(partial, got, send.at[7], recv.at[7], sibling)
    cross.start()
    pending.append(cross.wait_send)
    messages(dot(dmat[...], right[...]), m_dl)
    to_cells(m_dl, b_dl, send.at[4], recv.at[4], r, c)
    pending.append(lambda: sent(m_r, send.at[4], r, c))
    part = dot(dmat[:, ours], left[...], ((0,), (0,)))
    share(0)
    cross.wait_recv()
    natural_messages(part + got[...].astype(F32), m_dr)
    to_cells(m_dr, b_dr, send.at[5], recv.at[5], r, c)
    pending.append(lambda: sent(m_r, send.at[5], r, c))

    def back(n, lo, f):
        def body(q, _):
            at = pl.ds(pl.multiple_of(q * 128, 128), 128)
            d = f[pl.ds(q, 128, stride=8), :]
            dpb[lo:lo + 128, at] = (d * gate[q, lo:lo + 128]).astype(BF)
            dgb[lo:lo + 128, at] = (d * slope[q, lo:lo + 128]).astype(BF)
            return 0

        lax.fori_loop(0, 8, body, 0, unroll=4)
        s_src[n, pl.ds(0, 8)] = dot(xb[...], dpb[lo:lo + 128, :], ((1,), (1,))).reshape(8, 16, 128).astype(BF)
        s_src[n, pl.ds(8, 8)] = dot(xb[...], dgb[lo:lo + 128, :], ((1,), (1,))).reshape(8, 16, 128).astype(BF)
        scatter(n)

    arrived(b_dl, recv.at[4])
    f_left[...] = b_dl[...].astype(F32).reshape(1024, 128)
    back(1, 0, f_left)
    gather(0)
    arrived(b_dr, recv.at[5])
    f_right[...] = b_dr[...].astype(F32).reshape(1024, 128)
    back(2, 128, f_right)
    share(1)

    def last(q, _):
        at = pl.ds(pl.multiple_of(q * 128, 128), 128)
        dx = dot(w_proj[...], dpb[:, at]) + dot(w_gin[...], dgb[:, at]) + dot(w_gout[...], dsb[:, at])
        x_f = xh[q]
        dx = dx - jnp.mean(dx, axis=0, keepdims=True) - x_f * jnp.mean(dx * x_f, axis=0, keepdims=True)
        u = (ctt[q] + rstd[q][:1] * dx).astype(BF)
        gpair[pl.ds(q * 4, 4)] = dot(u, eye, ((0,), (0,))).astype(BF).reshape(4, 32, 128)
        return 0

    lax.fori_loop(0, 4, last, 0, unroll=2)
    share(2)
    gather(1)
    lax.fori_loop(4, 8, last, 0, unroll=2)
    put(gpair, gpair_h, 1)

    def total(n):
        arrived(s_out.at[n], recv.at[14 + n])
        s_sum[n] = s_out[n].astype(F32)
        put(s_sum.at[n], sums_h.at[n], 2 + n)

    total(0)
    gather(2)
    total(1)
    for wait in pending:
        wait()
    total(2)
    for copy in outs:
        copy.wait()


def finish(upd, gpair, sums, upd_o, gpair_o, g_proj, g_gin, g_gout, g_out, upd_v, gpair_v, sums_v, sem):
    loads = [
        pltpu.make_async_copy(a, b, sem.at[n])
        for n, (a, b) in enumerate([(upd, upd_v), (gpair, gpair_v), (sums, sums_v)])
    ]
    for copy in loads:
        copy.start()
    flat = sums_v.reshape(6, 128, 128)
    left, right = pl.ds(0, 128), pl.ds(128, 128)
    pairs = [
        (upd_v, upd_o), (gpair_v, gpair_o), (flat.at[0], g_gout), (flat.at[1], g_out),
        (flat.at[2], g_proj.at[:, left]), (flat.at[3], g_gin.at[:, left]),
        (flat.at[4], g_proj.at[:, right]), (flat.at[5], g_gin.at[:, right]),
    ]
    stores = [pltpu.make_async_copy(a, b, sem.at[3 + n]) for n, (a, b) in enumerate(pairs)]
    for n, copy in enumerate(stores):
        if n < 3:
            loads[n].wait()
        copy.start()
    for copy in stores:
        copy.wait()


def shards(pair, cotangent, chain_counts, crop_skip, w_proj, w_gate_in, w_gate_out, w_out):
    hbm = pl.BlockSpec(memory_space=pl.ANY)
    v = pltpu.VMEM
    s = jax.ShapeDtypeStruct
    scratch = (
        [pltpu.SMEM((4,), jnp.int32)] * 2 + [v((32, 32, 128), BF)] * 2
        + [v((128, 256), BF)] * 2 + [v((128, 128), BF)] * 2 + [v((32, 32, 128), BF)] * 2
        + [v((256, 128), BF), v((256, 128), BF), v((128, 128), BF), v((128, 128), BF), v((512, 512), BF)]
        + [v((8, 128, 128), F32), v((128, 1024), BF), v((8, 8, 128), F32), v((8, 128, 128), F32), v((8, 128, 128), F32)]
        + [v((8, 256, 128), F32), v((8, 256, 128), F32)]
        + [v((8, 128, 128), F32)] * 3
        + [v((128, 1024), BF)] * 3
        + [v((256, 1024), BF)] * 2
        + [v((1024, 128), F32)] * 2
        + [v((1024, 128), F32), v((256, 512), BF), v((512, 512), BF), v((256, 512), BF)]
        + [v((256, 512), BF)] * 2
        + [v((128, 8, 128), BF)] * 2 + [v((8, 16, 8, 128), BF)] + [v((128, 8, 128), BF)] + [v((8, 16, 8, 128), BF)] * 2
        + [v((8, 16, 8, 128), BF)] * 2 + [v((128, 8, 128), BF)] + [v((8, 16, 8, 128), BF)] + [v((128, 8, 128), BF)] * 2
        + [v((3, 16, 16, 128), BF)] * 2 + [v((3, 16, 128), BF), v((3, 16, 16, 128), BF), v((3, 16, 128), BF)]
        + [v((3, 16, 16, 128), BF), v((3, 16, 16, 128), F32)]
        + [pltpu.SemaphoreType.DMA((17,)), pltpu.SemaphoreType.DMA((17,)), pltpu.SemaphoreType.DMA((13,))]
        + [pltpu.SemaphoreType.REGULAR((1,))]
    )
    block = s((32, 32, 128), BF)
    wide, square = s((128, 256), F32), s((128, 128), F32)
    results = pl.pallas_call(
        kernel,
        out_shape=(block, block, s((3, 16, 16, 128), F32)),
        in_specs=[hbm] * 8,
        out_specs=(hbm,) * 3,
        scratch_shapes=scratch,
        compiler_params=pltpu.CompilerParams(collective_id=1, has_side_effects=True, vmem_limit_bytes=60 << 20),
    )(chain_counts, crop_skip, pair, cotangent, w_proj, w_gate_in, w_gate_out, w_out)
    return pl.pallas_call(
        finish,
        out_shape=(block, block, wide, wide, square, square),
        in_specs=[hbm] * 3,
        out_specs=(hbm,) * 6,
        scratch_shapes=[v(block.shape, BF)] * 2 + [v((3, 16, 16, 128), F32), pltpu.SemaphoreType.DMA((11,))],
        compiler_params=pltpu.CompilerParams(vmem_limit_bytes=60 << 20),
    )(*results)


def solution(mesh):
    in_specs = (P("row", "col", None), P("row", "col", None), P(), P(), P(), P(), P(), P())
    out_specs = (P("row", "col", None), P("row", "col", None), P(), P(), P(), P())
    return jax.shard_map(shards, mesh=mesh, in_specs=in_specs, out_specs=out_specs, check_vma=False)
```

```python
import jax
import jax.numpy as jnp
from jax import lax
from jax.experimental import pallas as pl
from jax.experimental.pallas import tpu as pltpu
from jax.sharding import PartitionSpec as P

MESH = pl.DeviceIdType.MESH
BF = jnp.bfloat16
F32 = jnp.float32
EPS = 1e-05


def dot(a, b, dims=((1,), (0,))):
    return lax.dot_general(a, b, (dims, ((), ())), preferred_element_type=F32)


def greet(r, c):
    barrier = pltpu.get_barrier_semaphore()
    half, m, core = r // 8, c // 2, lax.rem(c, 2)

    def body(s, _):
        dxh, dxl, dy = far_first(s >> 3)
        z = ((r >> 1) + 1 + s) & 3
        c2 = other_chip(m, dxl, dy) * 2 + (core ^ 1 ^ ((s >> 2) & 1))
        device = (core * 8 + z * 2 + ((r & 1) ^ dxh), c2)
        pl.semaphore_signal(barrier, inc=1, device_id=device, device_id_type=MESH)
        return 0

    lax.fori_loop(0, 127, body, 0)

    @pl.when(core != half)
    def _():
        pl.semaphore_signal(barrier, inc=1, device_id=(core * 8 + lax.rem(r, 8), c), device_id_type=MESH)


def greeted(r, c):
    barrier = pltpu.get_barrier_semaphore()
    same = r // 8 == lax.rem(c, 2)

    @pl.when(same)
    def _():
        pl.semaphore_wait(barrier, 127)

    @pl.when(jnp.logical_not(same))
    def _():
        pl.semaphore_wait(barrier, 128)


def remote(src, dst, send, recv, device):
    return pltpu.make_async_remote_copy(
        src_ref=src, dst_ref=dst, send_sem=send, recv_sem=recv, device_id=device, device_id_type=MESH
    )


def arrived(buf, sem):
    pltpu.make_async_copy(buf, buf, sem).wait()


def far_first(u):
    y = u >> 2
    dy = jnp.where(y == 0, 2, jnp.where(y == 1, 1, jnp.where(y == 2, 3, 0)))
    return 1 - (u & 1), 1 - ((u >> 1) & 1), dy


def other_chip(m, dx, dy):
    return (((m >> 2) ^ dx) << 2) + (((m & 3) + dy) & 3)


def far_z(r, t):
    k = (t + 1) >> 1
    return ((r >> 1) + jnp.where((t & 1) == 1, 4 - k, 4 + k)) & 7


def parity(r):
    return (r >> 1) & 1


def place(r):
    return ((r >> 2) & 1) * 2 + (r & 1)


def to_channels(src, dst, send, recv, r, c):
    half, m, core = r // 8, c // 2, lax.rem(c, 2)
    own = r * 8 + m

    def body(s, _):
        dxh, dxl, dy = far_first(s >> 3)
        r2 = far_z(r, s & 7) * 2 + ((r & 1) ^ dxh)
        m2 = other_chip(m, dxl, dy)
        remote(src.at[r2 * 8 + m2], dst, send, recv, (r2, m2 * 2 + half)).start()
        return 0

    lax.fori_loop(0, 127, body, 0)

    @pl.when(core == half)
    def _():
        pltpu.make_async_copy(src.at[own], dst, recv).start()

    @pl.when(core != half)
    def _():
        remote(src.at[own], dst, send, recv, (r, m * 2 + half)).start()


def to_cells(src, dst, group, send, recv, r, c):
    half, m, core = r // 8, c // 2, lax.rem(c, 2)
    channel = r * 8 + m
    mine = place(r)
    base = core * 8 + group * 2

    def body(s, _):
        _, dxl, dy = far_first((s >> 3) * 2)
        w = mine ^ 3 ^ (s & 3)
        c2 = other_chip(m, dxl, dy) * 2 + (core ^ 1 ^ ((s >> 2) & 1))
        remote(src.at[w, c2], dst.at[channel], send, recv, (base + (w >> 1) * 4 + (w & 1), c2)).start()
        return 0

    lax.fori_loop(0, 63, body, 0)
    to_self = jnp.logical_and(core == half, parity(r) == group)

    @pl.when(to_self)
    def _():
        pltpu.make_async_copy(src.at[mine, c], dst.at[channel], recv).start()

    @pl.when(jnp.logical_not(to_self))
    def _():
        remote(src.at[mine, c], dst.at[channel], send, recv, (base + (mine >> 1) * 4 + (mine & 1), c)).start()


def sent(src, send, r, c):
    same = r // 8 == lax.rem(c, 2)

    @pl.when(same)
    def _():
        arrived(src.at[pl.ds(0, 127)], send)

    @pl.when(jnp.logical_not(same))
    def _():
        arrived(src, send)


def sent_half(group, src, send, r, c):
    to_self = jnp.logical_and(lax.rem(c, 2) == r // 8, parity(r) == group)

    @pl.when(to_self)
    def _():
        arrived(src.at[pl.ds(0, 63)], send)

    @pl.when(jnp.logical_not(to_self))
    def _():
        arrived(src.at[pl.ds(0, 64)], send)


def along_plane(pick, dst, send, recv, r, c):
    core, m = c & 1, c >> 1
    me = (r & 1) * 16 + c
    pltpu.make_async_copy(pick(me), dst.at[me], recv).start()

    def body(s, _):
        dxh, dxl, dy = far_first(s >> 1)
        r2 = r ^ dxh
        c2 = other_chip(m, dxl, dy) * 2 + (core ^ 1 ^ (s & 1))
        remote(pick((r2 & 1) * 16 + c2), dst.at[me], send, recv, (r2, c2)).start()
        return 0

    lax.fori_loop(0, 31, body, 0)


def along_z(src, dst, send, recv, r, c):
    pltpu.make_async_copy(src, dst.at[r >> 1], recv).start()

    def body(s, _):
        remote(src, dst.at[r >> 1], send, recv, (far_z(r, s) * 2 + (r & 1), c)).start()
        return 0

    lax.fori_loop(0, 7, body, 0)


def valid_of(place, counts, skip):
    start = jnp.int32(0)
    valid = jnp.zeros(place.shape, F32)
    for n in range(counts.shape[0]):
        end = start + counts[n]
        inside = (place >= start) & (place < end) & (place - start >= skip[n])
        valid = jnp.where(inside, 1.0, valid)
        start = end
    return valid


def kernel(
    counts_h, skip_h, pair_h, cot_h, w_proj_h, w_gin_h, w_gout_h, w_out_h,
    upd_h, gpair_h, sums_h,
    counts, skip, pair, cot, w_proj, w_gin, w_gout, w_out, upd, gpair,
    wp_t, wg_t, wgo_t, wo_t, perm,
    xh, xb, rstd, pt, ctt, dxl, gate, slope, go, dgo, dtn, dyb, tnb, dsb, dpb, dgb,
    f_left, f_right, f_mat, left, right, dmat, partial, got,
    m_r, m_l, m_t, m_d, m_dl, m_dr,
    b_r, b_l, b_t, b_d, b_dl, b_dr,
    s_src, s_got, s_part, s_parts, s_tot, s_out, s_sum,
    send, recv, load,
):
    pending = []

    r, c = lax.axis_index("row"), lax.axis_index("col")
    core = lax.rem(c, 2)
    sibling = (r, c + 1 - 2 * core)
    loads = [
        pltpu.make_async_copy(a, b, load.at[n])
        for n, (a, b) in enumerate([
            (pair_h, pair), (w_proj_h, w_proj), (w_gin_h, w_gin), (counts_h, counts), (skip_h, skip),
            (cot_h, cot), (w_gout_h, w_gout), (w_out_h, w_out),
        ])
    ]
    for copy in loads:
        copy.start()
    greet(r, c)
    i0 = lax.broadcasted_iota(jnp.int32, (128, 128), 0)
    i1 = lax.broadcasted_iota(jnp.int32, (128, 128), 1)
    eye = jnp.where(i0 == i1, 1.0, 0.0).astype(BF)
    for copy in loads[:5]:
        copy.wait()
    wp_t[...] = w_proj[...].astype(F32).T.astype(BF)
    wg_t[...] = w_gin[...].astype(F32).T.astype(BF)

    def normed(q, _):
        p = pair[pl.ds(q * 4, 4)].reshape(128, 128)
        p_t = dot(eye, p, ((1,), (1,)))
        pt[q] = p_t
        mean = jnp.mean(p_t, axis=0, keepdims=True)
        dev = p_t - mean
        var = jnp.mean(dev * dev, axis=0, keepdims=True)
        rs = 1.0 / jnp.sqrt(var + EPS)
        x_f = dev * rs
        xh[q] = x_f
        rstd[q] = jnp.broadcast_to(rs, (8, 128))
        xb[:, pl.ds(pl.multiple_of(q * 128, 128), 128)] = x_f.astype(BF)
        return 0

    def project(lo, f):
        def body(q, _):
            x = xb[:, pl.ds(pl.multiple_of(q * 128, 128), 128)]
            s = dot(wp_t[lo:lo + 128, :], x)
            sig = jax.nn.sigmoid(dot(wg_t[lo:lo + 128, :], x))
            lane = lax.broadcasted_iota(jnp.int32, (1, 128), 1)
            mask = valid_of(r * 32 + q * 4 + lane // 32, counts, skip) * valid_of(c * 32 + lane % 32, counts, skip)
            open_ = mask * sig
            both = open_ * s
            gate[q, lo:lo + 128] = open_
            slope[q, lo:lo + 128] = both * (1.0 - sig)
            f[pl.ds(q, 128, stride=8), :] = both
            return 0

        lax.fori_loop(0, 8, body, 0, unroll=4)

    lax.fori_loop(0, 8, normed, 0, unroll=4)
    project(128, f_right)
    m_r[...] = f_right[...].reshape(128, 8, 128).astype(BF)
    greeted(r, c)
    group, spot = parity(r), place(r)
    to_channels(m_r, b_r.at[r & 7, c], send.at[0], recv.at[0], r, c)
    pending.append(lambda: sent(m_r, send.at[0], r, c))
    j0 = lax.broadcasted_iota(jnp.int32, (512, 512), 0)
    j1 = lax.broadcasted_iota(jnp.int32, (512, 512), 1)
    swapped = ((j0 >> 5) & 3) * 128 + (j0 >> 7) * 32 + (j0 & 31)
    perm[...] = jnp.where(swapped == j1, 1.0, 0.0).astype(BF)
    project(0, f_left)
    m_l[...] = f_left[...].reshape(128, 8, 128).astype(BF)

    @pl.when(group == 0)
    def _():
        to_channels(m_l, b_l.at[0, spot, c], send.at[1], recv.at[1], r, c)

    def before(q, _):
        at = pl.ds(pl.multiple_of(q * 128, 128), 128)
        ct = dot(eye, cot[pl.ds(q * 4, 4)].reshape(128, 128), ((1,), (1,)))
        ctt[q] = ct
        g = jax.nn.sigmoid(dot(wgo_t[...], xb[:, at]))
        go[q] = g
        dy_f = ct * g
        dgo[q] = dy_f * (1.0 - g)
        dy = dy_f.astype(BF)
        dyb[:, at] = dy
        dt = dot(w_out[...], dy)
        dtn[q] = dt - jnp.mean(dt, axis=0, keepdims=True)
        return 0


    for copy in loads[5:]:
        copy.wait()
    wgo_t[...] = w_gout[...].astype(F32).T.astype(BF)
    wo_t[...] = w_out[...].astype(F32).T.astype(BF)
    lax.fori_loop(0, 8, before, 0, unroll=2)

    @pl.when(group == 1)
    def _():
        to_channels(m_l, b_l.at[1, spot, c], send.at[1], recv.at[2], r, c)

    pending.append(lambda: sent(m_r, send.at[1], r, c))

    def turned(buf):
        n_rows = buf.shape[0] * 8
        rows = []
        for g in range(4):
            cols = [buf[:, 4 * g + n].astype(F32).reshape(n_rows, 128).astype(BF) for n in range(4)]
            rows.append(jnp.concatenate(cols, axis=1))
        return dot(jnp.concatenate(rows, axis=0), perm[...])

    def natural(buf, out):
        o = turned(buf)
        for g in range(4):
            for a in range(4):
                f_mat[pl.ds(g * 256 + a, 64, stride=4), :] = o[g * 64:(g + 1) * 64, a * 128:(a + 1) * 128]
        for g in range(4):
            out[:, g * 128:(g + 1) * 128] = f_mat[g * 256:(g + 1) * 256].astype(BF)

    def matrix(buf, out):
        o = turned(buf)
        for g in range(4):
            for a in range(4):
                out[a * 32:(a + 1) * 32, g * 128:(g + 1) * 128] = o[g * 32:(g + 1) * 32, a * 128:(a + 1) * 128].astype(BF)

    def spread(block):
        rows = [jnp.concatenate([block(a, g).astype(BF) for a in range(4)], axis=1) for g in range(4)]
        return dot(jnp.concatenate(rows, axis=0), perm[...])

    def messages(mat, out):
        o = spread(lambda a, g: mat[a * 32:(a + 1) * 32, g * 128:(g + 1) * 128])
        for g in range(4):
            for n in range(4):
                out[:, 4 * g + n] = o[g * 32:(g + 1) * 32, n * 128:(n + 1) * 128].reshape(4, 8, 128).astype(BF)

    def natural_messages(mat, out):
        for g in range(4):
            f_mat[g * 256:(g + 1) * 256] = mat[:, g * 128:(g + 1) * 128]
        o = spread(lambda a, g: f_mat[pl.ds(g * 256 + a, 64, stride=4), :])
        for g in range(4):
            for n in range(4):
                p = o[g * 64:(g + 1) * 64, n * 128:(n + 1) * 128].reshape(2, 2, 2, 8, 128).astype(BF)
                for x in range(2):
                    out[x, :, 4 * g + n] = p[:, x].reshape(4, 8, 128)

    def scatter(n):
        along_plane(lambda k: s_src.at[n, k], s_got.at[n], send.at[8 + n], recv.at[10 + n], r, c)
        pending.append(lambda: arrived(s_got.at[n, pl.ds(0, 31)], send.at[8 + n]))

    def share(n):
        arrived(s_got.at[n], recv.at[10 + n])
        s_part[n] = jnp.sum(s_got[n].astype(F32), axis=0).astype(BF)
        along_z(s_part.at[n], s_parts.at[n], send.at[11 + n], recv.at[13 + n], r, c)
        pending.append(lambda: arrived(s_parts.at[n, pl.ds(0, 7)], send.at[11 + n]))

    def gather(n):
        arrived(s_parts.at[n], recv.at[13 + n])
        s_tot[n] = (jnp.sum(s_parts[n].astype(F32), axis=0) * (1.0 / 512)).astype(BF)
        along_plane(lambda k: s_tot.at[n], s_out.at[n], send.at[14 + n], recv.at[16 + n], r, c)
        pending.append(lambda: arrived(s_got.at[n, pl.ds(0, 31)], send.at[14 + n]))

    outs = []

    def put(src, dst, n):
        copy = pltpu.make_async_copy(src, dst, load.at[8 + n])
        copy.start()
        outs.append(copy)

    mine = right.at[pl.ds(pl.multiple_of(core * 256, 256), 256)]
    arrived(b_r, recv.at[0])
    natural(b_r, mine)
    swap = remote(mine, mine, send.at[6], recv.at[8], sibling)
    swap.start()
    pending.append(swap.wait_send)
    for x in range(2):
        arrived(b_l.at[x], recv.at[1 + x])
        at = pl.ds(x * 128, 128)
        matrix(b_l.at[x], left.at[at])
        if x == 0:
            swap.wait_recv()
        messages(dot(left[at], right[...], ((1,), (1,))), m_t.at[x])
        to_cells(m_t.at[x], b_t, x, send.at[2 + 15 * x], recv.at[3], r, c)
    pending.append(lambda: sent_half(1, m_r, send.at[17], r, c))
    pending.append(lambda: sent_half(0, m_r, send.at[2], r, c))
    pending.append(lambda: sent(m_r, send.at[4], r, c))
    arrived(b_t, recv.at[3])
    f_left[...] = b_t[...].astype(F32).reshape(1024, 128)

    def middle(q, _):
        at = pl.ds(pl.multiple_of(q * 128, 128), 128)
        t = f_left[pl.ds(q, 128, stride=8), :]
        dev = t - jnp.mean(t, axis=0, keepdims=True)
        rs = 1.0 / jnp.sqrt(jnp.mean(dev * dev, axis=0, keepdims=True) + EPS)
        that = dev * rs
        tnb[:, at] = that.astype(BF)
        d = dtn[q]
        f_right[pl.ds(q, 128, stride=8), :] = rs * (d - that * jnp.mean(d * that, axis=0, keepdims=True))
        return 0

    lax.fori_loop(0, 8, middle, 0, unroll=4)
    m_d[...] = f_right[...].reshape(128, 8, 128).astype(BF)
    to_channels(m_d, b_d.at[group, spot, c], send.at[3], recv.at[4 + group], r, c)
    pending.append(lambda: sent(m_r, send.at[3], r, c))

    def after(q, _):
        at = pl.ds(pl.multiple_of(q * 128, 128), 128)
        y = dot(wo_t[...], tnb[:, at])
        dsb[:, at] = (dgo[q] * y).astype(BF)
        u = (pt[q] + go[q] * y).astype(BF)
        upd[pl.ds(q * 4, 4)] = dot(u, eye, ((0,), (0,))).astype(BF).reshape(4, 32, 128)
        return 0

    theirs = pl.ds(pl.multiple_of((1 - core) * 256, 256), 256)
    ours = pl.ds(pl.multiple_of(core * 256, 256), 256)
    cross = remote(partial, got, send.at[7], recv.at[9], sibling)
    for x in range(2):
        arrived(b_d.at[x], recv.at[4 + x])
        at = pl.ds(x * 128, 128)
        matrix(b_d.at[x], dmat.at[at])
        if x == 1:
            partial[...] = dot(dmat[:, theirs], left[...], ((0,), (0,))).astype(BF)
            cross.start()
        messages(dot(dmat[at], right[...]), m_dl.at[x])
        to_cells(m_dl.at[x], b_dl, x, send.at[4], recv.at[6], r, c)
    pending.append(cross.wait_send)
    part = dot(dmat[:, ours], left[...], ((0,), (0,)))
    cross.wait_recv()
    natural_messages(part + got[...].astype(F32), m_dr)
    for x in range(2):
        to_cells(m_dr.at[x], b_dr, x, send.at[5], recv.at[7], r, c)
    pending.append(lambda: sent(m_r, send.at[5], r, c))
    lax.fori_loop(0, 8, after, 0, unroll=2)
    put(upd, upd_h, 0)
    s_src[0, pl.ds(0, 16)] = dot(xb[...], dsb[...], ((1,), (1,))).reshape(16, 8, 128).astype(BF)
    s_src[0, pl.ds(16, 16)] = dot(tnb[...], dyb[...], ((1,), (1,))).reshape(16, 8, 128).astype(BF)
    scatter(0)

    def back(n, lo, f):
        def body(q, _):
            at = pl.ds(pl.multiple_of(q * 128, 128), 128)
            d = f[pl.ds(q, 128, stride=8), :]
            dpb[lo:lo + 128, at] = (d * gate[q, lo:lo + 128]).astype(BF)
            dgb[lo:lo + 128, at] = (d * slope[q, lo:lo + 128]).astype(BF)
            return 0

        lax.fori_loop(0, 8, body, 0, unroll=4)
        s_src[n, pl.ds(0, 16)] = dot(xb[...], dpb[lo:lo + 128, :], ((1,), (1,))).reshape(16, 8, 128).astype(BF)
        s_src[n, pl.ds(16, 16)] = dot(xb[...], dgb[lo:lo + 128, :], ((1,), (1,))).reshape(16, 8, 128).astype(BF)
        scatter(n)

    arrived(b_dl, recv.at[6])
    f_left[...] = b_dl[...].astype(F32).reshape(1024, 128)
    back(1, 0, f_left)

    def early(q, _):
        at = pl.ds(pl.multiple_of(q * 128, 128), 128)
        dxl[q] = (
            dot(w_proj[:, :128], dpb[:128, at]) + dot(w_gin[:, :128], dgb[:128, at]) + dot(w_gout[...], dsb[:, at])
        )
        return 0

    lax.fori_loop(0, 8, early, 0, unroll=2)
    arrived(b_dr, recv.at[7])
    f_right[...] = b_dr[...].astype(F32).reshape(1024, 128)
    back(2, 128, f_right)
    share(0)
    share(1)

    def last(q, _):
        at = pl.ds(pl.multiple_of(q * 128, 128), 128)
        dx = dxl[q] + dot(w_proj[:, 128:], dpb[128:, at]) + dot(w_gin[:, 128:], dgb[128:, at])
        x_f = xh[q]
        dx = dx - jnp.mean(dx, axis=0, keepdims=True) - x_f * jnp.mean(dx * x_f, axis=0, keepdims=True)
        u = (ctt[q] + rstd[q][:1] * dx).astype(BF)
        gpair[pl.ds(q * 4, 4)] = dot(u, eye, ((0,), (0,))).astype(BF).reshape(4, 32, 128)
        return 0

    lax.fori_loop(0, 2, last, 0, unroll=2)
    share(2)
    gather(0)
    gather(1)
    lax.fori_loop(2, 6, last, 0, unroll=2)

    def total(n):
        arrived(s_out.at[n], recv.at[16 + n])
        s_sum[n] = s_out[n].astype(F32)
        put(s_sum.at[n], sums_h.at[n], 2 + n)

    gather(2)
    lax.fori_loop(6, 8, last, 0, unroll=2)
    put(gpair, gpair_h, 1)
    total(0)
    total(1)
    for wait in pending:
        wait()
    total(2)
    for copy in outs:
        copy.wait()


def finish(upd, gpair, sums, upd_o, gpair_o, g_proj, g_gin, g_gout, g_out, upd_v, gpair_v, sums_v, sem):
    loads = [
        pltpu.make_async_copy(a, b, sem.at[n])
        for n, (a, b) in enumerate([(upd, upd_v), (gpair, gpair_v), (sums, sums_v)])
    ]
    for copy in loads:
        copy.start()
    flat = sums_v.reshape(6, 128, 128)
    left, right = pl.ds(0, 128), pl.ds(128, 128)
    pairs = [
        (upd_v, upd_o), (gpair_v, gpair_o), (flat.at[0], g_gout), (flat.at[1], g_out),
        (flat.at[2], g_proj.at[:, left]), (flat.at[3], g_gin.at[:, left]),
        (flat.at[4], g_proj.at[:, right]), (flat.at[5], g_gin.at[:, right]),
    ]
    stores = [pltpu.make_async_copy(a, b, sem.at[3 + n]) for n, (a, b) in enumerate(pairs)]
    for n, copy in enumerate(stores):
        if n < 3:
            loads[n].wait()
        copy.start()
    for copy in stores:
        copy.wait()


def shards(pair, cotangent, chain_counts, crop_skip, w_proj, w_gate_in, w_gate_out, w_out):
    hbm = pl.BlockSpec(memory_space=pl.ANY)
    v = pltpu.VMEM
    s = jax.ShapeDtypeStruct
    scratch = (
        [pltpu.SMEM((4,), jnp.int32)] * 2 + [v((32, 32, 128), BF)] * 2
        + [v((128, 256), BF)] * 2 + [v((128, 128), BF)] * 2 + [v((32, 32, 128), BF)] * 2
        + [v((256, 128), BF), v((256, 128), BF), v((128, 128), BF), v((128, 128), BF), v((512, 512), BF)]
        + [v((8, 128, 128), F32), v((128, 1024), BF), v((8, 8, 128), F32), v((8, 128, 128), F32), v((8, 128, 128), F32)]
        + [v((8, 128, 128), F32)]
        + [v((8, 256, 128), F32), v((8, 256, 128), F32)]
        + [v((8, 128, 128), F32)] * 3
        + [v((128, 1024), BF)] * 3
        + [v((256, 1024), BF)] * 2
        + [v((1024, 128), F32)] * 2
        + [v((1024, 128), F32), v((256, 512), BF), v((512, 512), BF), v((256, 512), BF)]
        + [v((256, 512), BF)] * 2
        + [v((128, 8, 128), BF)] * 2 + [v((2, 4, 16, 8, 128), BF)] + [v((128, 8, 128), BF)] + [v((2, 4, 16, 8, 128), BF)] * 2
        + [v((8, 16, 8, 128), BF), v((2, 4, 16, 8, 128), BF), v((128, 8, 128), BF), v((2, 4, 16, 8, 128), BF)]
        + [v((128, 8, 128), BF)] * 2
        + [v((3, 32, 8, 128), BF)] * 2 + [v((3, 8, 128), BF), v((3, 8, 8, 128), BF), v((3, 8, 128), BF)]
        + [v((3, 32, 8, 128), BF), v((3, 32, 8, 128), F32)]
        + [pltpu.SemaphoreType.DMA((18,)), pltpu.SemaphoreType.DMA((19,)), pltpu.SemaphoreType.DMA((13,))]
    )
    block = s((32, 32, 128), BF)
    wide, square = s((128, 256), F32), s((128, 128), F32)
    results = pl.pallas_call(
        kernel,
        out_shape=(block, block, s((3, 32, 8, 128), F32)),
        in_specs=[hbm] * 8,
        out_specs=(hbm,) * 3,
        scratch_shapes=scratch,
        compiler_params=pltpu.CompilerParams(collective_id=1, has_side_effects=True, vmem_limit_bytes=60 << 20),
    )(chain_counts, crop_skip, pair, cotangent, w_proj, w_gate_in, w_gate_out, w_out)
    return pl.pallas_call(
        finish,
        out_shape=(block, block, wide, wide, square, square),
        in_specs=[hbm] * 3,
        out_specs=(hbm,) * 6,
        scratch_shapes=[v(block.shape, BF)] * 2 + [v((3, 32, 8, 128), F32), pltpu.SemaphoreType.DMA((11,))],
        compiler_params=pltpu.CompilerParams(vmem_limit_bytes=60 << 20),
    )(*results)


def solution(mesh):
    in_specs = (P("row", "col", None), P("row", "col", None), P(), P(), P(), P(), P(), P())
    out_specs = (P("row", "col", None), P("row", "col", None), P(), P(), P(), P())
    return jax.shard_map(shards, mesh=mesh, in_specs=in_specs, out_specs=out_specs, check_vma=False)
```

```python
import jax
import jax.numpy as jnp
from jax import lax
from jax.experimental import pallas as pl
from jax.experimental.pallas import tpu as pltpu
from jax.sharding import PartitionSpec as P

MESH = pl.DeviceIdType.MESH
BF = jnp.bfloat16
F32 = jnp.float32
EPS = 1e-05


def dot(a, b, dims=((1,), (0,))):
    return lax.dot_general(a, b, (dims, ((), ())), preferred_element_type=F32)


def greet(r, c):
    barrier = pltpu.get_barrier_semaphore()
    half, m, core = r // 8, c // 2, lax.rem(c, 2)

    def body(s, _):
        dxh, dxl, dy = far_first(s >> 3)
        z = ((r >> 1) + 1 + s) & 3
        c2 = other_chip(m, dxl, dy) * 2 + (core ^ 1 ^ ((s >> 2) & 1))
        device = (core * 8 + z * 2 + ((r & 1) ^ dxh), c2)
        pl.semaphore_signal(barrier, inc=1, device_id=device, device_id_type=MESH)
        return 0

    lax.fori_loop(0, 127, body, 0)

    @pl.when(core != half)
    def _():
        pl.semaphore_signal(barrier, inc=1, device_id=(core * 8 + lax.rem(r, 8), c), device_id_type=MESH)


def greeted(r, c):
    barrier = pltpu.get_barrier_semaphore()
    same = r // 8 == lax.rem(c, 2)

    @pl.when(same)
    def _():
        pl.semaphore_wait(barrier, 127)

    @pl.when(jnp.logical_not(same))
    def _():
        pl.semaphore_wait(barrier, 128)


def remote(src, dst, send, recv, device):
    return pltpu.make_async_remote_copy(
        src_ref=src, dst_ref=dst, send_sem=send, recv_sem=recv, device_id=device, device_id_type=MESH
    )


def arrived(buf, sem):
    pltpu.make_async_copy(buf, buf, sem).wait()


def far_first(u):
    y = u >> 2
    dy = jnp.where(y == 0, 2, jnp.where(y == 1, 1, jnp.where(y == 2, 3, 0)))
    return 1 - (u & 1), 1 - ((u >> 1) & 1), dy


def other_chip(m, dx, dy):
    return (((m >> 2) ^ dx) << 2) + (((m & 3) + dy) & 3)


def far_z(r, t):
    k = (t + 1) >> 1
    return ((r >> 1) + jnp.where((t & 1) == 1, 4 - k, 4 + k)) & 7


def parity(r):
    return (r >> 1) & 1


def place(r):
    return ((r >> 2) & 1) * 2 + (r & 1)


def to_channels(src, dst, send, recv, r, c):
    half, m, core = r // 8, c // 2, lax.rem(c, 2)
    own = r * 8 + m

    def body(s, _):
        dxh, dxl, dy = far_first(s >> 3)
        r2 = far_z(r, s & 7) * 2 + ((r & 1) ^ dxh)
        m2 = other_chip(m, dxl, dy)
        remote(src.at[r2 * 8 + m2], dst, send, recv, (r2, m2 * 2 + half)).start()
        return 0

    lax.fori_loop(0, 127, body, 0)

    @pl.when(core == half)
    def _():
        pltpu.make_async_copy(src.at[own], dst, recv).start()

    @pl.when(core != half)
    def _():
        remote(src.at[own], dst, send, recv, (r, m * 2 + half)).start()


def to_cells(src, dst, group, send, recv, r, c):
    half, m, core = r // 8, c // 2, lax.rem(c, 2)
    channel = r * 8 + m
    mine = place(r)
    base = core * 8 + group * 2

    def body(s, _):
        _, dxl, dy = far_first((s >> 3) * 2)
        w = mine ^ 3 ^ (s & 3)
        c2 = other_chip(m, dxl, dy) * 2 + (core ^ 1 ^ ((s >> 2) & 1))
        remote(src.at[w, c2], dst.at[channel], send, recv, (base + (w >> 1) * 4 + (w & 1), c2)).start()
        return 0

    lax.fori_loop(0, 63, body, 0)
    to_self = jnp.logical_and(core == half, parity(r) == group)

    @pl.when(to_self)
    def _():
        pltpu.make_async_copy(src.at[mine, c], dst.at[channel], recv).start()

    @pl.when(jnp.logical_not(to_self))
    def _():
        remote(src.at[mine, c], dst.at[channel], send, recv, (base + (mine >> 1) * 4 + (mine & 1), c)).start()


def sent(src, send, r, c):
    same = r // 8 == lax.rem(c, 2)

    @pl.when(same)
    def _():
        arrived(src.at[pl.ds(0, 127)], send)

    @pl.when(jnp.logical_not(same))
    def _():
        arrived(src, send)


def sent_half(group, src, send, r, c):
    to_self = jnp.logical_and(lax.rem(c, 2) == r // 8, parity(r) == group)

    @pl.when(to_self)
    def _():
        arrived(src.at[pl.ds(0, 63)], send)

    @pl.when(jnp.logical_not(to_self))
    def _():
        arrived(src.at[pl.ds(0, 64)], send)


def along_plane(pick, dst, send, recv, r, c):
    core, m = c & 1, c >> 1
    me = (r & 1) * 16 + c
    pltpu.make_async_copy(pick(me), dst.at[me], recv).start()

    def body(s, _):
        dxh, dxl, dy = far_first(s >> 1)
        r2 = r ^ dxh
        c2 = other_chip(m, dxl, dy) * 2 + (core ^ 1 ^ (s & 1))
        remote(pick((r2 & 1) * 16 + c2), dst.at[me], send, recv, (r2, c2)).start()
        return 0

    lax.fori_loop(0, 31, body, 0)


def to_plane(src, dst, send, recv, r, c):
    me = (r & 1) * 16 + c
    pltpu.make_async_copy(src, dst.at[me], recv).start()

    def body(s, _):
        k = s + jnp.where(s >= (me ^ 1), 1, 0)
        p = k ^ 1
        remote(src, dst.at[me], send, recv, ((r & 14) + (p >> 4), p & 15)).start()
        return 0

    lax.fori_loop(0, 31, body, 0)


def along_z(src, dst, send, recv, r, c):
    pltpu.make_async_copy(src, dst.at[r >> 1], recv).start()

    def body(s, _):
        z = s + jnp.where(s >= (r >> 1), 1, 0)
        remote(src, dst.at[r >> 1], send, recv, (z * 2 + (r & 1), c)).start()
        return 0

    lax.fori_loop(0, 7, body, 0)


def valid_of(place, counts, skip):
    start = jnp.int32(0)
    valid = jnp.zeros(place.shape, F32)
    for n in range(counts.shape[0]):
        end = start + counts[n]
        inside = (place >= start) & (place < end) & (place - start >= skip[n])
        valid = jnp.where(inside, 1.0, valid)
        start = end
    return valid


def kernel(
    counts_h, skip_h, pair_h, cot_h, w_proj_h, w_gin_h, w_gout_h, w_out_h,
    upd_h, gpair_h, sums_h,
    counts, skip, pair, cot, w_proj, w_gin, w_gout, w_out, upd, gpair,
    wp_t, wg_t, wgo_t, wo_t, perm,
    xh, xb, rstd, pt, ctt, dxl, gate, slope, go, dgo, dtn, dyb, tnb, dsb, dpb, dgb,
    f_left, f_right, f_mat, left, right, dmat, partial, got,
    m_r, m_l, m_t, m_d, m_dl, m_dr,
    b_r, b_l, b_t, b_d, b_dl, b_dr,
    a_src, a_got, a_part, a_parts, a_tot, a_out, s_src, s_got, s_part, s_parts, s_tot, s_out, s_sum,
    send, recv, load,
):
    pending = []
    groups = ((a_src, a_got, a_part, a_parts, a_tot, a_out), (s_src, s_got, s_part, s_parts, s_tot, s_out))

    r, c = lax.axis_index("row"), lax.axis_index("col")
    core = lax.rem(c, 2)
    sibling = (r, c + 1 - 2 * core)
    loads = [
        pltpu.make_async_copy(a, b, load.at[n])
        for n, (a, b) in enumerate([
            (pair_h, pair), (w_proj_h, w_proj), (w_gin_h, w_gin), (counts_h, counts), (skip_h, skip),
            (cot_h, cot), (w_gout_h, w_gout), (w_out_h, w_out),
        ])
    ]
    for copy in loads:
        copy.start()
    greet(r, c)
    i0 = lax.broadcasted_iota(jnp.int32, (128, 128), 0)
    i1 = lax.broadcasted_iota(jnp.int32, (128, 128), 1)
    eye = jnp.where(i0 == i1, 1.0, 0.0).astype(BF)
    for copy in loads[:5]:
        copy.wait()
    wp_t[...] = w_proj[...].astype(F32).T.astype(BF)
    wg_t[...] = w_gin[...].astype(F32).T.astype(BF)

    def normed(q, _):
        p = pair[pl.ds(q * 4, 4)].reshape(128, 128)
        p_t = dot(eye, p, ((1,), (1,)))
        pt[q] = p_t
        mean = jnp.mean(p_t, axis=0, keepdims=True)
        dev = p_t - mean
        var = jnp.mean(dev * dev, axis=0, keepdims=True)
        rs = 1.0 / jnp.sqrt(var + EPS)
        x_f = dev * rs
        xh[q] = x_f
        rstd[q] = jnp.broadcast_to(rs, (8, 128))
        xb[:, pl.ds(pl.multiple_of(q * 128, 128), 128)] = x_f.astype(BF)
        return 0

    def project(lo, f):
        def body(q, _):
            x = xb[:, pl.ds(pl.multiple_of(q * 128, 128), 128)]
            s = dot(wp_t[lo:lo + 128, :], x)
            sig = jax.nn.sigmoid(dot(wg_t[lo:lo + 128, :], x))
            lane = lax.broadcasted_iota(jnp.int32, (1, 128), 1)
            mask = valid_of(r * 32 + q * 4 + lane // 32, counts, skip) * valid_of(c * 32 + lane % 32, counts, skip)
            open_ = mask * sig
            both = open_ * s
            gate[q, lo:lo + 128] = open_
            slope[q, lo:lo + 128] = both * (1.0 - sig)
            f[pl.ds(q, 128, stride=8), :] = both
            return 0

        lax.fori_loop(0, 8, body, 0, unroll=4)

    lax.fori_loop(0, 8, normed, 0, unroll=4)
    project(128, f_right)
    m_r[...] = f_right[:1024].reshape(128, 8, 128).astype(BF)
    greeted(r, c)
    group, spot = parity(r), place(r)
    to_channels(m_r, b_r.at[r & 7, c], send.at[0], recv.at[0], r, c)
    pending.append(lambda: sent(m_r, send.at[0], r, c))
    j0 = lax.broadcasted_iota(jnp.int32, (512, 512), 0)
    j1 = lax.broadcasted_iota(jnp.int32, (512, 512), 1)
    swapped = ((j0 >> 5) & 3) * 128 + (j0 >> 7) * 32 + (j0 & 31)
    perm[...] = jnp.where(swapped == j1, 1.0, 0.0).astype(BF)
    project(0, f_left)
    m_l[...] = f_left[:1024].reshape(128, 8, 128).astype(BF)

    @pl.when(group == 0)
    def _():
        to_channels(m_l, b_l.at[0, spot, c], send.at[1], recv.at[1], r, c)

    def before(q, _):
        at = pl.ds(pl.multiple_of(q * 128, 128), 128)
        ct = dot(eye, cot[pl.ds(q * 4, 4)].reshape(128, 128), ((1,), (1,)))
        ctt[q] = ct
        g = jax.nn.sigmoid(dot(wgo_t[...], xb[:, at]))
        go[q] = g
        dy_f = ct * g
        dgo[q] = dy_f * (1.0 - g)
        dy = dy_f.astype(BF)
        dyb[:, at] = dy
        dt = dot(w_out[...], dy)
        dtn[q] = dt - jnp.mean(dt, axis=0, keepdims=True)
        return 0


    for copy in loads[5:]:
        copy.wait()
    wgo_t[...] = w_gout[...].astype(F32).T.astype(BF)
    wo_t[...] = w_out[...].astype(F32).T.astype(BF)
    lax.fori_loop(0, 8, before, 0, unroll=2)

    @pl.when(group == 1)
    def _():
        to_channels(m_l, b_l.at[1, spot, c], send.at[1], recv.at[2], r, c)

    pending.append(lambda: sent(m_r, send.at[1], r, c))

    def turned(buf):
        n_rows = buf.shape[0] * 8
        rows = []
        for g in range(4):
            cols = [buf[:, 4 * g + n].astype(F32).reshape(n_rows, 128).astype(BF) for n in range(4)]
            rows.append(jnp.concatenate(cols, axis=1))
        return dot(jnp.concatenate(rows, axis=0), perm[...])

    def natural(buf, out):
        o = turned(buf)
        for g in range(4):
            for a in range(4):
                f_mat[pl.ds(g * 256 + a, 64, stride=4), :] = o[g * 64:(g + 1) * 64, a * 128:(a + 1) * 128]
        for g in range(4):
            out[:, g * 128:(g + 1) * 128] = f_mat[g * 256:(g + 1) * 256].astype(BF)

    def matrix(buf, out):
        o = turned(buf)
        for g in range(4):
            for a in range(4):
                out[a * 32:(a + 1) * 32, g * 128:(g + 1) * 128] = o[g * 32:(g + 1) * 32, a * 128:(a + 1) * 128].astype(BF)

    def spread(block):
        rows = [jnp.concatenate([block(a, g).astype(BF) for a in range(4)], axis=1) for g in range(4)]
        return dot(jnp.concatenate(rows, axis=0), perm[...])

    def messages(mat, out):
        o = spread(lambda a, g: mat[a * 32:(a + 1) * 32, g * 128:(g + 1) * 128])
        for g in range(4):
            for n in range(4):
                out[:, 4 * g + n] = o[g * 32:(g + 1) * 32, n * 128:(n + 1) * 128].reshape(4, 8, 128).astype(BF)

    def natural_messages(mat, out):
        for g in range(4):
            f_mat[g * 256:(g + 1) * 256] = mat[:, g * 128:(g + 1) * 128]
        o = spread(lambda a, g: f_mat[pl.ds(g * 256 + a, 64, stride=4), :])
        for g in range(4):
            for n in range(4):
                p = o[g * 64:(g + 1) * 64, n * 128:(n + 1) * 128].reshape(2, 2, 2, 8, 128).astype(BF)
                for x in range(2):
                    out[x, :, 4 * g + n] = p[:, x].reshape(4, 8, 128)

    def scatter(n):
        src, got = groups[n][:2]
        along_plane(lambda k: src.at[k], got, send.at[8 + n], recv.at[10 + n], r, c)
        pending.append(lambda: arrived(got.at[pl.ds(0, 31)], send.at[8 + n]))

    def share(n):
        got, part, parts = groups[n][1:4]
        arrived(got, recv.at[10 + n])
        part[...] = jnp.sum(got[...].astype(F32), axis=0).astype(BF)
        along_z(part, parts, send.at[11 + n], recv.at[13 + n], r, c)
        pending.append(lambda: arrived(parts.at[pl.ds(0, 7)], send.at[11 + n]))

    def gather(n):
        parts, tot, out = groups[n][3:]
        arrived(parts, recv.at[13 + n])
        tot[...] = (jnp.sum(parts[...].astype(F32), axis=0) * (1.0 / 512)).astype(BF)
        to_plane(tot, out, send.at[14 + n], recv.at[16 + n], r, c)
        pending.append(lambda: arrived(out.at[pl.ds(0, 31)], send.at[14 + n]))

    outs = []

    def put(src, dst, n):
        copy = pltpu.make_async_copy(src, dst, load.at[8 + n])
        copy.start()
        outs.append(copy)

    mine = right.at[pl.ds(pl.multiple_of(core * 256, 256), 256)]
    arrived(b_r, recv.at[0])
    natural(b_r, mine)
    swap = remote(mine, mine, send.at[6], recv.at[8], sibling)
    swap.start()
    pending.append(swap.wait_send)
    for x in range(2):
        arrived(b_l.at[x], recv.at[1 + x])
        at = pl.ds(x * 128, 128)
        matrix(b_l.at[x], left.at[at])
        if x == 0:
            swap.wait_recv()
        messages(dot(left[at], right[...], ((1,), (1,))), m_t.at[x])
        to_cells(m_t.at[x], b_t, x, send.at[2 + 15 * x], recv.at[3], r, c)
    pending.append(lambda: sent_half(1, m_r, send.at[17], r, c))
    pending.append(lambda: sent_half(0, m_r, send.at[2], r, c))
    pending.append(lambda: sent(m_r, send.at[4], r, c))
    arrived(b_t, recv.at[3])
    f_left[:1024] = b_t[...].astype(F32).reshape(1024, 128)

    def middle(q, _):
        at = pl.ds(pl.multiple_of(q * 128, 128), 128)
        t = f_left[pl.ds(q, 128, stride=8), :]
        dev = t - jnp.mean(t, axis=0, keepdims=True)
        rs = 1.0 / jnp.sqrt(jnp.mean(dev * dev, axis=0, keepdims=True) + EPS)
        that = dev * rs
        tnb[:, at] = that.astype(BF)
        d = dtn[q]
        f_right[pl.ds(q, 128, stride=8), :] = rs * (d - that * jnp.mean(d * that, axis=0, keepdims=True))
        return 0

    lax.fori_loop(0, 8, middle, 0, unroll=4)
    m_d[...] = f_right[:1024].reshape(128, 8, 128).astype(BF)
    to_channels(m_d, b_d.at[group, spot, c], send.at[3], recv.at[4 + group], r, c)
    pending.append(lambda: sent(m_r, send.at[3], r, c))

    def after(q, _):
        at = pl.ds(pl.multiple_of(q * 128, 128), 128)
        y = dot(wo_t[...], tnb[:, at])
        dsb[:, at] = (dgo[q] * y).astype(BF)
        u = (pt[q] + go[q] * y).astype(BF)
        upd[pl.ds(q * 4, 4)] = dot(u, eye, ((0,), (0,))).astype(BF).reshape(4, 32, 128)
        return 0

    theirs = pl.ds(pl.multiple_of((1 - core) * 256, 256), 256)
    ours = pl.ds(pl.multiple_of(core * 256, 256), 256)
    cross = remote(partial, got, send.at[7], recv.at[9], sibling)
    for x in range(2):
        arrived(b_d.at[x], recv.at[4 + x])
        at = pl.ds(x * 128, 128)
        matrix(b_d.at[x], dmat.at[at])
        if x == 1:
            partial[...] = dot(dmat[:, theirs], left[...], ((0,), (0,))).astype(BF)
            cross.start()
        messages(dot(dmat[at], right[...]), m_dl.at[x])
        to_cells(m_dl.at[x], b_dl, x, send.at[4], recv.at[6], r, c)
    pending.append(cross.wait_send)
    part = dot(dmat[:, ours], left[...], ((0,), (0,)))
    cross.wait_recv()
    natural_messages(part + got[...].astype(F32), m_dr)
    for x in range(2):
        to_cells(m_dr.at[x], b_dr, x, send.at[5], recv.at[7], r, c)
    pending.append(lambda: sent(m_r, send.at[5], r, c))
    lax.fori_loop(0, 8, after, 0, unroll=2)
    put(upd, upd_h, 0)
    a_src[pl.ds(0, 16), 0] = dot(xb[...], dsb[...], ((1,), (1,))).reshape(16, 8, 128).astype(BF)
    a_src[pl.ds(16, 16), 0] = dot(tnb[...], dyb[...], ((1,), (1,))).reshape(16, 8, 128).astype(BF)
    def back(lo, f):
        def body(q, _):
            at = pl.ds(pl.multiple_of(q * 128, 128), 128)
            d = f[pl.ds(q, 128, stride=8), :]
            dpb[lo:lo + 128, at] = (d * gate[q, lo:lo + 128]).astype(BF)
            dgb[lo:lo + 128, at] = (d * slope[q, lo:lo + 128]).astype(BF)
            return 0

        lax.fori_loop(0, 8, body, 0, unroll=4)
        return tuple(
            dot(xb[...], d[lo:lo + 128, :], ((1,), (1,))).reshape(16, 8, 128).astype(BF) for d in (dpb, dgb)
        )

    arrived(b_dl, recv.at[6])
    f_left[:1024] = b_dl[...].astype(F32).reshape(1024, 128)
    a_src[pl.ds(0, 16), 1], a_src[pl.ds(16, 16), 1] = back(0, f_left)
    scatter(0)

    def early(q, _):
        at = pl.ds(pl.multiple_of(q * 128, 128), 128)
        dxl[q] = (
            dot(w_proj[:, :128], dpb[:128, at]) + dot(w_gin[:, :128], dgb[:128, at]) + dot(w_gout[...], dsb[:, at])
        )
        return 0

    lax.fori_loop(0, 8, early, 0, unroll=2)
    arrived(b_dr, recv.at[7])
    f_right[:1024] = b_dr[...].astype(F32).reshape(1024, 128)
    s_src[pl.ds(0, 16)], s_src[pl.ds(16, 16)] = back(128, f_right)
    scatter(1)
    share(0)

    def last(q, _):
        at = pl.ds(pl.multiple_of(q * 128, 128), 128)
        dx = dxl[q] + dot(w_proj[:, 128:], dpb[128:, at]) + dot(w_gin[:, 128:], dgb[128:, at])
        x_f = xh[q]
        dx = dx - jnp.mean(dx, axis=0, keepdims=True) - x_f * jnp.mean(dx * x_f, axis=0, keepdims=True)
        u = (ctt[q] + rstd[q][:1] * dx).astype(BF)
        gpair[pl.ds(q * 4, 4)] = dot(u, eye, ((0,), (0,))).astype(BF).reshape(4, 32, 128)
        return 0

    lax.fori_loop(0, 2, last, 0, unroll=2)
    share(1)
    gather(0)
    lax.fori_loop(2, 6, last, 0, unroll=2)

    gather(1)
    lax.fori_loop(6, 8, last, 0, unroll=2)
    put(gpair, gpair_h, 1)
    arrived(a_out, recv.at[16])
    for n in range(2):
        s_sum[n] = a_out[:, n].astype(F32)
        put(s_sum.at[n], sums_h.at[n], 2 + n)
    for wait in pending:
        wait()
    arrived(s_out, recv.at[17])
    s_sum[2] = s_out[...].astype(F32)
    put(s_sum.at[2], sums_h.at[2], 4)
    for copy in outs:
        copy.wait()


def finish(upd, gpair, sums, upd_o, gpair_o, g_proj, g_gin, g_gout, g_out, upd_v, gpair_v, sums_v, sem):
    loads = [
        pltpu.make_async_copy(a, b, sem.at[n])
        for n, (a, b) in enumerate([(upd, upd_v), (gpair, gpair_v), (sums, sums_v)])
    ]
    for copy in loads:
        copy.start()
    flat = sums_v.reshape(6, 128, 128)
    left, right = pl.ds(0, 128), pl.ds(128, 128)
    pairs = [
        (upd_v, upd_o), (gpair_v, gpair_o), (flat.at[0], g_gout), (flat.at[1], g_out),
        (flat.at[2], g_proj.at[:, left]), (flat.at[3], g_gin.at[:, left]),
        (flat.at[4], g_proj.at[:, right]), (flat.at[5], g_gin.at[:, right]),
    ]
    stores = [pltpu.make_async_copy(a, b, sem.at[3 + n]) for n, (a, b) in enumerate(pairs)]
    for n, copy in enumerate(stores):
        if n < 3:
            loads[n].wait()
        copy.start()
    for copy in stores:
        copy.wait()


def shards(pair, cotangent, chain_counts, crop_skip, w_proj, w_gate_in, w_gate_out, w_out):
    hbm = pl.BlockSpec(memory_space=pl.ANY)
    v = pltpu.VMEM
    s = jax.ShapeDtypeStruct
    scratch = (
        [pltpu.SMEM((4,), jnp.int32)] * 2 + [v((32, 32, 128), BF)] * 2
        + [v((128, 256), BF)] * 2 + [v((128, 128), BF)] * 2 + [v((32, 32, 128), BF)] * 2
        + [v((256, 128), BF), v((256, 128), BF), v((128, 128), BF), v((128, 128), BF), v((512, 512), BF)]
        + [v((8, 128, 128), F32), v((128, 1024), BF), v((8, 8, 128), F32), v((8, 128, 128), F32), v((8, 128, 128), F32)]
        + [v((8, 128, 128), F32)]
        + [v((8, 256, 128), F32), v((8, 256, 128), F32)]
        + [v((8, 128, 128), F32)] * 3
        + [v((128, 1024), BF)] * 3
        + [v((256, 1024), BF)] * 2
        + [v((1032, 128), F32)] * 2
        + [v((1032, 128), F32), v((256, 512), BF), v((512, 512), BF), v((256, 512), BF)]
        + [v((256, 512), BF)] * 2
        + [v((128, 8, 128), BF)] * 2 + [v((2, 4, 16, 8, 128), BF)] + [v((128, 8, 128), BF)] + [v((2, 4, 16, 8, 128), BF)] * 2
        + [v((8, 16, 8, 128), BF), v((2, 4, 16, 8, 128), BF), v((128, 8, 128), BF), v((2, 4, 16, 8, 128), BF)]
        + [v((128, 8, 128), BF)] * 2
        + [v((32, 2, 8, 128), BF)] * 2 + [v((2, 8, 128), BF), v((8, 2, 8, 128), BF), v((2, 8, 128), BF)]
        + [v((32, 2, 8, 128), BF)] + [v((32, 8, 128), BF)] * 2
        + [v((8, 128), BF), v((8, 8, 128), BF), v((8, 128), BF), v((32, 8, 128), BF), v((3, 32, 8, 128), F32)]
        + [pltpu.SemaphoreType.DMA((18,)), pltpu.SemaphoreType.DMA((19,)), pltpu.SemaphoreType.DMA((13,))]
    )
    block = s((32, 32, 128), BF)
    wide, square = s((128, 256), F32), s((128, 128), F32)
    results = pl.pallas_call(
        kernel,
        out_shape=(block, block, s((3, 32, 8, 128), F32)),
        in_specs=[hbm] * 8,
        out_specs=(hbm,) * 3,
        scratch_shapes=scratch,
        compiler_params=pltpu.CompilerParams(collective_id=1, has_side_effects=True, vmem_limit_bytes=60 << 20),
    )(chain_counts, crop_skip, pair, cotangent, w_proj, w_gate_in, w_gate_out, w_out)
    return pl.pallas_call(
        finish,
        out_shape=(block, block, wide, wide, square, square),
        in_specs=[hbm] * 3,
        out_specs=(hbm,) * 6,
        scratch_shapes=[v(block.shape, BF)] * 2 + [v((3, 32, 8, 128), F32), pltpu.SemaphoreType.DMA((11,))],
        compiler_params=pltpu.CompilerParams(vmem_limit_bytes=60 << 20),
    )(*results)


def solution(mesh):
    in_specs = (P("row", "col", None), P("row", "col", None), P(), P(), P(), P(), P(), P())
    out_specs = (P("row", "col", None), P("row", "col", None), P(), P(), P(), P())
    return jax.shard_map(shards, mesh=mesh, in_specs=in_specs, out_specs=out_specs, check_vma=False)
```

```python
import jax
import jax.numpy as jnp
from jax import lax
from jax.experimental import pallas as pl
from jax.experimental.pallas import tpu as pltpu
from jax.sharding import PartitionSpec as P

MESH = pl.DeviceIdType.MESH
BF = jnp.bfloat16
F32 = jnp.float32
EPS = 1e-05


def dot(a, b, dims=((1,), (0,))):
    return lax.dot_general(a, b, (dims, ((), ())), preferred_element_type=F32)


def greet(r, c):
    barrier = pltpu.get_barrier_semaphore()
    half, m, core = r // 8, c // 2, lax.rem(c, 2)

    def body(s, _):
        dxh, dxl, dy = far_first(s >> 3)
        z = ((r >> 1) + 1 + s) & 3
        c2 = other_chip(m, dxl, dy) * 2 + (core ^ 1 ^ ((s >> 2) & 1))
        device = (core * 8 + z * 2 + ((r & 1) ^ dxh), c2)
        pl.semaphore_signal(barrier, inc=1, device_id=device, device_id_type=MESH)
        return 0

    lax.fori_loop(0, 127, body, 0)

    @pl.when(core != half)
    def _():
        pl.semaphore_signal(barrier, inc=1, device_id=(core * 8 + lax.rem(r, 8), c), device_id_type=MESH)


def greeted(r, c):
    barrier = pltpu.get_barrier_semaphore()
    same = r // 8 == lax.rem(c, 2)

    @pl.when(same)
    def _():
        pl.semaphore_wait(barrier, 127)

    @pl.when(jnp.logical_not(same))
    def _():
        pl.semaphore_wait(barrier, 128)


def remote(src, dst, send, recv, device):
    return pltpu.make_async_remote_copy(
        src_ref=src, dst_ref=dst, send_sem=send, recv_sem=recv, device_id=device, device_id_type=MESH
    )


def arrived(buf, sem):
    pltpu.make_async_copy(buf, buf, sem).wait()


def far_first(u):
    y = u >> 2
    dy = jnp.where(y == 0, 2, jnp.where(y == 1, 1, jnp.where(y == 2, 3, 0)))
    return 1 - (u & 1), 1 - ((u >> 1) & 1), dy


def other_chip(m, dx, dy):
    return (((m >> 2) ^ dx) << 2) + (((m & 3) + dy) & 3)


def far_z(r, t):
    k = (t + 1) >> 1
    return ((r >> 1) + jnp.where((t & 1) == 1, 4 - k, 4 + k)) & 7


def parity(r):
    return (r >> 1) & 1


def place(r):
    return ((r >> 2) & 1) * 2 + (r & 1)


def to_channels(src, dst, send, recv, r, c):
    half, m, core = r // 8, c // 2, lax.rem(c, 2)
    own = r * 8 + m

    def body(s, _):
        dxh, dxl, dy = far_first(s >> 3)
        r2 = far_z(r, s & 7) * 2 + ((r & 1) ^ dxh)
        m2 = other_chip(m, dxl, dy)
        remote(src.at[r2 * 8 + m2], dst, send, recv, (r2, m2 * 2 + half)).start()
        return 0

    lax.fori_loop(0, 127, body, 0)

    @pl.when(core == half)
    def _():
        pltpu.make_async_copy(src.at[own], dst, recv).start()

    @pl.when(core != half)
    def _():
        remote(src.at[own], dst, send, recv, (r, m * 2 + half)).start()


def to_cells(src, dst, group, send, recv, r, c):
    half, m, core = r // 8, c // 2, lax.rem(c, 2)
    channel = r * 8 + m
    mine = place(r)
    base = core * 8 + group * 2

    def body(s, _):
        _, dxl, dy = far_first((s >> 3) * 2)
        w = mine ^ 3 ^ (s & 3)
        c2 = other_chip(m, dxl, dy) * 2 + (core ^ 1 ^ ((s >> 2) & 1))
        remote(src.at[w, c2], dst.at[channel], send, recv, (base + (w >> 1) * 4 + (w & 1), c2)).start()
        return 0

    lax.fori_loop(0, 63, body, 0)
    to_self = jnp.logical_and(core == half, parity(r) == group)

    @pl.when(to_self)
    def _():
        pltpu.make_async_copy(src.at[mine, c], dst.at[channel], recv).start()

    @pl.when(jnp.logical_not(to_self))
    def _():
        remote(src.at[mine, c], dst.at[channel], send, recv, (base + (mine >> 1) * 4 + (mine & 1), c)).start()


def sent(src, send, r, c):
    same = r // 8 == lax.rem(c, 2)

    @pl.when(same)
    def _():
        arrived(src.at[pl.ds(0, 127)], send)

    @pl.when(jnp.logical_not(same))
    def _():
        arrived(src, send)


def sent_half(group, src, send, r, c):
    to_self = jnp.logical_and(lax.rem(c, 2) == r // 8, parity(r) == group)

    @pl.when(to_self)
    def _():
        arrived(src.at[pl.ds(0, 63)], send)

    @pl.when(jnp.logical_not(to_self))
    def _():
        arrived(src.at[pl.ds(0, 64)], send)


def along_plane(pick, dst, send, recv, r, c):
    core, m = c & 1, c >> 1
    me = (r & 1) * 16 + c
    pltpu.make_async_copy(pick(me), dst.at[me], recv).start()

    def body(s, _):
        dxh, dxl, dy = far_first(s >> 1)
        r2 = r ^ dxh
        c2 = other_chip(m, dxl, dy) * 2 + (core ^ 1 ^ (s & 1))
        remote(pick((r2 & 1) * 16 + c2), dst.at[me], send, recv, (r2, c2)).start()
        return 0

    lax.fori_loop(0, 31, body, 0)


def to_plane(src, dst, send, recv, r, c):
    me = (r & 1) * 16 + c
    pltpu.make_async_copy(src, dst.at[me], recv).start()

    def body(s, _):
        k = s + jnp.where(s >= (me ^ 1), 1, 0)
        p = k ^ 1
        remote(src, dst.at[me], send, recv, ((r & 14) + (p >> 4), p & 15)).start()
        return 0

    lax.fori_loop(0, 31, body, 0)


def along_z(src, dst, send, recv, r, c):
    pltpu.make_async_copy(src, dst.at[r >> 1], recv).start()

    def body(s, _):
        z = s + jnp.where(s >= (r >> 1), 1, 0)
        remote(src, dst.at[r >> 1], send, recv, (z * 2 + (r & 1), c)).start()
        return 0

    lax.fori_loop(0, 7, body, 0)


def valid_of(place, counts, skip):
    start = jnp.int32(0)
    valid = jnp.zeros(place.shape, F32)
    for n in range(counts.shape[0]):
        end = start + counts[n]
        inside = (place >= start) & (place < end) & (place - start >= skip[n])
        valid = jnp.where(inside, 1.0, valid)
        start = end
    return valid


def kernel(
    counts_h, skip_h, pair_h, cot_h, w_proj_h, w_gin_h, w_gout_h, w_out_h,
    upd_h, gpair_h, sums_h,
    counts, skip, pair, cot, w_proj, w_gin, w_gout, w_out, upd, gpair,
    wp_t, wg_t, wgo_t, wo_t, perm,
    xh, xb, rstd, pt, ctt, dxl, gate, slope, go, dgo, dtn, dyb, tnb, dsb, dpb, dgb,
    f_left, f_right, f_mat, left, right, dmat, partial, got,
    m_r, m_l, m_t, m_d, m_dl, m_dr,
    b_r, b_l, b_t, b_d, b_dl, b_dr,
    a_src, a_got, a_part, a_parts, a_tot, a_out, s_src, s_got, s_part, s_parts, s_tot, s_out, s_sum,
    send, recv, load,
):
    pending = []
    groups = ((a_src, a_got, a_part, a_parts, a_tot, a_out), (s_src, s_got, s_part, s_parts, s_tot, s_out))

    r, c = lax.axis_index("row"), lax.axis_index("col")
    core = lax.rem(c, 2)
    sibling = (r, c + 1 - 2 * core)
    loads = [
        pltpu.make_async_copy(a, b, load.at[n])
        for n, (a, b) in enumerate([
            (pair_h, pair), (w_proj_h, w_proj), (w_gin_h, w_gin), (counts_h, counts), (skip_h, skip),
            (cot_h, cot), (w_gout_h, w_gout), (w_out_h, w_out),
        ])
    ]
    for copy in loads:
        copy.start()
    greet(r, c)
    i0 = lax.broadcasted_iota(jnp.int32, (128, 128), 0)
    i1 = lax.broadcasted_iota(jnp.int32, (128, 128), 1)
    eye = jnp.where(i0 == i1, 1.0, 0.0).astype(BF)
    for copy in loads[:5]:
        copy.wait()
    wp_t[...] = w_proj[...].astype(F32).T.astype(BF)
    wg_t[...] = w_gin[...].astype(F32).T.astype(BF)

    def normed(q, _):
        p = pair[pl.ds(q * 4, 4)].reshape(128, 128)
        p_t = dot(eye, p, ((1,), (1,)))
        pt[q] = p_t
        mean = jnp.mean(p_t, axis=0, keepdims=True)
        dev = p_t - mean
        var = jnp.mean(dev * dev, axis=0, keepdims=True)
        rs = 1.0 / jnp.sqrt(var + EPS)
        x_f = dev * rs
        xh[q] = x_f
        rstd[q] = jnp.broadcast_to(rs, (8, 128))
        xb[:, pl.ds(pl.multiple_of(q * 128, 128), 128)] = x_f.astype(BF)
        return 0

    def project(lo, f):
        def body(q, _):
            x = xb[:, pl.ds(pl.multiple_of(q * 128, 128), 128)]
            s = dot(wp_t[lo:lo + 128, :], x)
            sig = jax.nn.sigmoid(dot(wg_t[lo:lo + 128, :], x))
            lane = lax.broadcasted_iota(jnp.int32, (1, 128), 1)
            mask = valid_of(r * 32 + q * 4 + lane // 32, counts, skip) * valid_of(c * 32 + lane % 32, counts, skip)
            open_ = mask * sig
            both = open_ * s
            gate[q, lo:lo + 128] = open_
            slope[q, lo:lo + 128] = both * (1.0 - sig)
            f[pl.ds(q, 128, stride=8), :] = both
            return 0

        lax.fori_loop(0, 8, body, 0, unroll=4)

    lax.fori_loop(0, 8, normed, 0, unroll=4)
    project(128, f_right)
    m_r[...] = f_right[:1024].reshape(128, 8, 128).astype(BF)
    greeted(r, c)
    group, spot = parity(r), place(r)
    to_channels(m_r, b_r.at[r & 7, c], send.at[0], recv.at[0], r, c)
    pending.append(lambda: sent(m_r, send.at[0], r, c))
    j0 = lax.broadcasted_iota(jnp.int32, (512, 512), 0)
    j1 = lax.broadcasted_iota(jnp.int32, (512, 512), 1)
    swapped = ((j0 >> 5) & 3) * 128 + (j0 >> 7) * 32 + (j0 & 31)
    perm[...] = jnp.where(swapped == j1, 1.0, 0.0).astype(BF)
    project(0, f_left)
    m_l[...] = f_left[:1024].reshape(128, 8, 128).astype(BF)

    to_channels(m_l, b_l.at[group, spot, c], send.at[1], recv.at[1 + group], r, c)
    pending.append(lambda: sent(m_r, send.at[1], r, c))

    def before(q, _):
        at = pl.ds(pl.multiple_of(q * 128, 128), 128)
        ct = dot(eye, cot[pl.ds(q * 4, 4)].reshape(128, 128), ((1,), (1,)))
        ctt[q] = ct
        g = jax.nn.sigmoid(dot(wgo_t[...], xb[:, at]))
        go[q] = g
        dy_f = ct * g
        dgo[q] = dy_f * (1.0 - g)
        dy = dy_f.astype(BF)
        dyb[:, at] = dy
        dt = dot(w_out[...], dy)
        dtn[q] = dt - jnp.mean(dt, axis=0, keepdims=True)
        return 0


    def turned(buf):
        n_rows = buf.shape[0] * 8
        rows = []
        for g in range(4):
            cols = [buf[:, 4 * g + n].astype(F32).reshape(n_rows, 128).astype(BF) for n in range(4)]
            rows.append(jnp.concatenate(cols, axis=1))
        return dot(jnp.concatenate(rows, axis=0), perm[...])

    def natural(buf, out):
        o = turned(buf)
        for g in range(4):
            for a in range(4):
                f_mat[pl.ds(g * 256 + a, 64, stride=4), :] = o[g * 64:(g + 1) * 64, a * 128:(a + 1) * 128]
        for g in range(4):
            out[:, g * 128:(g + 1) * 128] = f_mat[g * 256:(g + 1) * 256].astype(BF)

    def matrix(buf, out):
        o = turned(buf)
        for g in range(4):
            for a in range(4):
                out[a * 32:(a + 1) * 32, g * 128:(g + 1) * 128] = o[g * 32:(g + 1) * 32, a * 128:(a + 1) * 128].astype(BF)

    def spread(block):
        rows = [jnp.concatenate([block(a, g).astype(BF) for a in range(4)], axis=1) for g in range(4)]
        return dot(jnp.concatenate(rows, axis=0), perm[...])

    def messages(mat, out):
        o = spread(lambda a, g: mat[a * 32:(a + 1) * 32, g * 128:(g + 1) * 128])
        for g in range(4):
            for n in range(4):
                out[:, 4 * g + n] = o[g * 32:(g + 1) * 32, n * 128:(n + 1) * 128].reshape(4, 8, 128).astype(BF)

    def natural_messages(mat, out):
        for g in range(4):
            f_mat[g * 256:(g + 1) * 256] = mat[:, g * 128:(g + 1) * 128]
        o = spread(lambda a, g: f_mat[pl.ds(g * 256 + a, 64, stride=4), :])
        for g in range(4):
            for n in range(4):
                p = o[g * 64:(g + 1) * 64, n * 128:(n + 1) * 128].reshape(2, 2, 2, 8, 128).astype(BF)
                for x in range(2):
                    out[x, :, 4 * g + n] = p[:, x].reshape(4, 8, 128)

    def scatter(n):
        src, got = groups[n][:2]
        along_plane(lambda k: src.at[k], got, send.at[8 + n], recv.at[10 + n], r, c)
        pending.append(lambda: arrived(got.at[pl.ds(0, 31)], send.at[8 + n]))

    def share(n):
        got, part, parts = groups[n][1:4]
        arrived(got, recv.at[10 + n])
        part[...] = jnp.sum(got[...].astype(F32), axis=0).astype(BF)
        along_z(part, parts, send.at[11 + n], recv.at[13 + n], r, c)
        pending.append(lambda: arrived(parts.at[pl.ds(0, 7)], send.at[11 + n]))

    def gather(n):
        parts, tot, out = groups[n][3:]
        arrived(parts, recv.at[13 + n])
        tot[...] = (jnp.sum(parts[...].astype(F32), axis=0) * (1.0 / 512)).astype(BF)
        to_plane(tot, out, send.at[14 + n], recv.at[16 + n], r, c)
        pending.append(lambda: arrived(out.at[pl.ds(0, 31)], send.at[14 + n]))

    outs = []

    def put(src, dst, n):
        copy = pltpu.make_async_copy(src, dst, load.at[8 + n])
        copy.start()
        outs.append(copy)

    mine = right.at[pl.ds(pl.multiple_of(core * 256, 256), 256)]
    arrived(b_r, recv.at[0])
    natural(b_r, mine)
    swap = remote(mine, mine, send.at[6], recv.at[8], sibling)
    swap.start()
    pending.append(swap.wait_send)

    for copy in loads[5:]:
        copy.wait()
    wgo_t[...] = w_gout[...].astype(F32).T.astype(BF)
    wo_t[...] = w_out[...].astype(F32).T.astype(BF)
    lax.fori_loop(0, 8, before, 0, unroll=2)
    for x in range(2):
        arrived(b_l.at[x], recv.at[1 + x])
        at = pl.ds(x * 128, 128)
        matrix(b_l.at[x], left.at[at])
        if x == 0:
            swap.wait_recv()
        messages(dot(left[at], right[...], ((1,), (1,))), m_t.at[x])
        to_cells(m_t.at[x], b_t, x, send.at[2 + 15 * x], recv.at[3], r, c)
    pending.append(lambda: sent_half(1, m_r, send.at[17], r, c))
    pending.append(lambda: sent_half(0, m_r, send.at[2], r, c))
    pending.append(lambda: sent(m_r, send.at[4], r, c))
    arrived(b_t, recv.at[3])
    f_left[:1024] = b_t[...].astype(F32).reshape(1024, 128)

    def middle(q, _):
        at = pl.ds(pl.multiple_of(q * 128, 128), 128)
        t = f_left[pl.ds(q, 128, stride=8), :]
        dev = t - jnp.mean(t, axis=0, keepdims=True)
        rs = 1.0 / jnp.sqrt(jnp.mean(dev * dev, axis=0, keepdims=True) + EPS)
        that = dev * rs
        tnb[:, at] = that.astype(BF)
        d = dtn[q]
        f_right[pl.ds(q, 128, stride=8), :] = rs * (d - that * jnp.mean(d * that, axis=0, keepdims=True))
        return 0

    lax.fori_loop(0, 8, middle, 0, unroll=4)
    m_d[...] = f_right[:1024].reshape(128, 8, 128).astype(BF)
    to_channels(m_d, b_d.at[group, spot, c], send.at[3], recv.at[4 + group], r, c)
    pending.append(lambda: sent(m_r, send.at[3], r, c))

    def after(q, _):
        at = pl.ds(pl.multiple_of(q * 128, 128), 128)
        y = dot(wo_t[...], tnb[:, at])
        dsb[:, at] = (dgo[q] * y).astype(BF)
        u = (pt[q] + go[q] * y).astype(BF)
        upd[pl.ds(q * 4, 4)] = dot(u, eye, ((0,), (0,))).astype(BF).reshape(4, 32, 128)
        return 0

    theirs = pl.ds(pl.multiple_of((1 - core) * 256, 256), 256)
    ours = pl.ds(pl.multiple_of(core * 256, 256), 256)
    cross = remote(partial, got, send.at[7], recv.at[9], sibling)
    for x in range(2):
        arrived(b_d.at[x], recv.at[4 + x])
        at = pl.ds(x * 128, 128)
        matrix(b_d.at[x], dmat.at[at])
        if x == 1:
            partial[...] = dot(dmat[:, theirs], left[...], ((0,), (0,))).astype(BF)
            cross.start()
        messages(dot(dmat[at], right[...]), m_dl.at[x])
        to_cells(m_dl.at[x], b_dl, x, send.at[4], recv.at[6], r, c)
    pending.append(cross.wait_send)
    part = dot(dmat[:, ours], left[...], ((0,), (0,)))
    cross.wait_recv()
    natural_messages(part + got[...].astype(F32), m_dr)
    for x in range(2):
        to_cells(m_dr.at[x], b_dr, x, send.at[5], recv.at[7], r, c)
    pending.append(lambda: sent(m_r, send.at[5], r, c))
    lax.fori_loop(0, 8, after, 0, unroll=2)
    put(upd, upd_h, 0)
    a_src[pl.ds(0, 16), 0] = dot(xb[...], dsb[...], ((1,), (1,))).reshape(16, 8, 128).astype(BF)
    a_src[pl.ds(16, 16), 0] = dot(tnb[...], dyb[...], ((1,), (1,))).reshape(16, 8, 128).astype(BF)
    def back(lo, f):
        def body(q, _):
            at = pl.ds(pl.multiple_of(q * 128, 128), 128)
            d = f[pl.ds(q, 128, stride=8), :]
            dpb[lo:lo + 128, at] = (d * gate[q, lo:lo + 128]).astype(BF)
            dgb[lo:lo + 128, at] = (d * slope[q, lo:lo + 128]).astype(BF)
            return 0

        lax.fori_loop(0, 8, body, 0, unroll=4)
        return tuple(
            dot(xb[...], d[lo:lo + 128, :], ((1,), (1,))).reshape(16, 8, 128).astype(BF) for d in (dpb, dgb)
        )

    arrived(b_dl, recv.at[6])
    f_left[:1024] = b_dl[...].astype(F32).reshape(1024, 128)
    a_src[pl.ds(0, 16), 1], a_src[pl.ds(16, 16), 1] = back(0, f_left)
    scatter(0)

    def early(q, _):
        at = pl.ds(pl.multiple_of(q * 128, 128), 128)
        dxl[q] = (
            dot(w_proj[:, :128], dpb[:128, at]) + dot(w_gin[:, :128], dgb[:128, at]) + dot(w_gout[...], dsb[:, at])
        )
        return 0

    lax.fori_loop(0, 8, early, 0, unroll=2)
    arrived(b_dr, recv.at[7])
    f_right[:1024] = b_dr[...].astype(F32).reshape(1024, 128)
    s_src[pl.ds(0, 16)], s_src[pl.ds(16, 16)] = back(128, f_right)
    scatter(1)
    share(0)

    def last(q, _):
        at = pl.ds(pl.multiple_of(q * 128, 128), 128)
        dx = dxl[q] + dot(w_proj[:, 128:], dpb[128:, at]) + dot(w_gin[:, 128:], dgb[128:, at])
        x_f = xh[q]
        dx = dx - jnp.mean(dx, axis=0, keepdims=True) - x_f * jnp.mean(dx * x_f, axis=0, keepdims=True)
        u = (ctt[q] + rstd[q][:1] * dx).astype(BF)
        gpair[pl.ds(q * 4, 4)] = dot(u, eye, ((0,), (0,))).astype(BF).reshape(4, 32, 128)
        return 0

    lax.fori_loop(0, 2, last, 0, unroll=2)
    share(1)
    gather(0)
    lax.fori_loop(2, 6, last, 0, unroll=2)

    gather(1)
    lax.fori_loop(6, 8, last, 0, unroll=2)
    put(gpair, gpair_h, 1)
    arrived(a_out, recv.at[16])
    for n in range(2):
        s_sum[n] = a_out[:, n].astype(F32)
        put(s_sum.at[n], sums_h.at[n], 2 + n)
    for wait in pending:
        wait()
    arrived(s_out, recv.at[17])
    s_sum[2] = s_out[...].astype(F32)
    put(s_sum.at[2], sums_h.at[2], 4)
    for copy in outs:
        copy.wait()


def finish(upd, gpair, sums, upd_o, gpair_o, g_proj, g_gin, g_gout, g_out, upd_v, gpair_v, sums_v, sem):
    loads = [
        pltpu.make_async_copy(a, b, sem.at[n])
        for n, (a, b) in enumerate([(upd, upd_v), (gpair, gpair_v), (sums, sums_v)])
    ]
    for copy in loads:
        copy.start()
    flat = sums_v.reshape(6, 128, 128)
    left, right = pl.ds(0, 128), pl.ds(128, 128)
    pairs = [
        (upd_v, upd_o), (gpair_v, gpair_o), (flat.at[0], g_gout), (flat.at[1], g_out),
        (flat.at[2], g_proj.at[:, left]), (flat.at[3], g_gin.at[:, left]),
        (flat.at[4], g_proj.at[:, right]), (flat.at[5], g_gin.at[:, right]),
    ]
    stores = [pltpu.make_async_copy(a, b, sem.at[3 + n]) for n, (a, b) in enumerate(pairs)]
    for n, copy in enumerate(stores):
        if n < 3:
            loads[n].wait()
        copy.start()
    for copy in stores:
        copy.wait()


def shards(pair, cotangent, chain_counts, crop_skip, w_proj, w_gate_in, w_gate_out, w_out):
    hbm = pl.BlockSpec(memory_space=pl.ANY)
    v = pltpu.VMEM
    s = jax.ShapeDtypeStruct
    scratch = (
        [pltpu.SMEM((4,), jnp.int32)] * 2 + [v((32, 32, 128), BF)] * 2
        + [v((128, 256), BF)] * 2 + [v((128, 128), BF)] * 2 + [v((32, 32, 128), BF)] * 2
        + [v((256, 128), BF), v((256, 128), BF), v((128, 128), BF), v((128, 128), BF), v((512, 512), BF)]
        + [v((8, 128, 128), F32), v((128, 1024), BF), v((8, 8, 128), F32), v((8, 128, 128), F32), v((8, 128, 128), F32)]
        + [v((8, 128, 128), F32)]
        + [v((8, 256, 128), F32), v((8, 256, 128), F32)]
        + [v((8, 128, 128), F32)] * 3
        + [v((128, 1024), BF)] * 3
        + [v((256, 1024), BF)] * 2
        + [v((1032, 128), F32)] * 2
        + [v((1032, 128), F32), v((256, 512), BF), v((512, 512), BF), v((256, 512), BF)]
        + [v((256, 512), BF)] * 2
        + [v((128, 8, 128), BF)] * 2 + [v((2, 4, 16, 8, 128), BF)] + [v((128, 8, 128), BF)] + [v((2, 4, 16, 8, 128), BF)] * 2
        + [v((8, 16, 8, 128), BF), v((2, 4, 16, 8, 128), BF), v((128, 8, 128), BF), v((2, 4, 16, 8, 128), BF)]
        + [v((128, 8, 128), BF)] * 2
        + [v((32, 2, 8, 128), BF)] * 2 + [v((2, 8, 128), BF), v((8, 2, 8, 128), BF), v((2, 8, 128), BF)]
        + [v((32, 2, 8, 128), BF)] + [v((32, 8, 128), BF)] * 2
        + [v((8, 128), BF), v((8, 8, 128), BF), v((8, 128), BF), v((32, 8, 128), BF), v((3, 32, 8, 128), F32)]
        + [pltpu.SemaphoreType.DMA((18,)), pltpu.SemaphoreType.DMA((19,)), pltpu.SemaphoreType.DMA((13,))]
    )
    block = s((32, 32, 128), BF)
    wide, square = s((128, 256), F32), s((128, 128), F32)
    results = pl.pallas_call(
        kernel,
        out_shape=(block, block, s((3, 32, 8, 128), F32)),
        in_specs=[hbm] * 8,
        out_specs=(hbm,) * 3,
        scratch_shapes=scratch,
        compiler_params=pltpu.CompilerParams(collective_id=1, has_side_effects=True, vmem_limit_bytes=60 << 20),
    )(chain_counts, crop_skip, pair, cotangent, w_proj, w_gate_in, w_gate_out, w_out)
    return pl.pallas_call(
        finish,
        out_shape=(block, block, wide, wide, square, square),
        in_specs=[hbm] * 3,
        out_specs=(hbm,) * 6,
        scratch_shapes=[v(block.shape, BF)] * 2 + [v((3, 32, 8, 128), F32), pltpu.SemaphoreType.DMA((11,))],
        compiler_params=pltpu.CompilerParams(vmem_limit_bytes=60 << 20),
    )(*results)


def solution(mesh):
    in_specs = (P("row", "col", None), P("row", "col", None), P(), P(), P(), P(), P(), P())
    out_specs = (P("row", "col", None), P("row", "col", None), P(), P(), P(), P())
    return jax.shard_map(shards, mesh=mesh, in_specs=in_specs, out_specs=out_specs, check_vma=False)
```
